128 devices in a mesh: pts: 8 (over x, core), ca: 4 (over y), cb: 4 (over z).
Axes of the slice: x: 4, y: 4, z: 4, core: 2. Of those that a mesh axis runs over, the one named last changes fastest.
Arguments:
- points: bfloat16 [131072, 1024], P(('pts', 'ca', 'cb')), may hold values from -6 to 6
- candidates: bfloat16 [12288, 1024], P(('ca', 'cb')), may hold values from -0.1875 to 0.1875
- probes: int32 [1024, 24], P(('pts', 'ca', 'cb')), may hold values from 0 to 95, all different within a row
- chosen: int32 [4], replicated, may hold values from 0 to 12287
Outputs:
- facility_gains: float32 [4, 12288], P(None, ('ca', 'cb'))
- coverage: float32 [131072], P(('pts', 'ca', 'cb'))
The draws below stay inside these ranges and needn't reach their ends.
Inputs may be any that keep to these rules, and one draw needn't show every extreme that they name: `probes`: the 24 entries of a row are distinct; every candidate block is probed by some point block.
All inputs are finite; a program needn't handle non-finite values.
Results may differ from the reference program's by a relative error of at most 0.0003.
Values may be sent and summed in bfloat16 or wider, within the bound.
A program may use at most 128 MiB of HBM per device.

```python
import jax
import jax.numpy as jnp
from jax import lax

D = 1024
BLK = 128
PROBES = 24
STEPS = 4
PB_DEV = 8
NPB = 1024
NCB = 96


def place_ends(drawn, rng, least, largest):
    longest = drawn.shape.index(max(drawn.shape))
    spots = []
    for shift in (0, 1):
        where = [jax.random.randint(jax.random.fold_in(rng, axis), (), 0, length) for axis, length in enumerate(drawn.shape)]
        where[longest] = (where[longest] + shift) % drawn.shape[longest]
        spots.append(tuple(where))
    return drawn.at[spots[0]].set(least).at[spots[1]].set(largest)


def steps_of(own_key, dims, split, smallest, largest):
    loudness = 1.0
    for dim, parts in split:
        draws = jax.random.uniform(jax.random.fold_in(jax.random.fold_in(own_key, 6), dim), (parts,), jnp.float32, smallest / len(split), largest / len(split))
        loudness = loudness * jnp.repeat(jnp.exp(draws), dims[dim] // parts).reshape((-1,) + (1,) * (len(dims) - 1 - dim))
    return loudness


def picks_of(rng, rows, amount, top, lift):
    order = jax.random.permutation(jax.random.fold_in(rng, 1), amount)
    favour = order
    for power in range(3):
        favour = favour * favour // amount
    favour = favour * lift // amount
    lots = jax.random.randint(jax.random.fold_in(rng, 2), (rows, amount), 0, 4096) + favour
    holders = jax.random.permutation(jax.random.fold_in(rng, 3), rows)[jnp.arange(amount) % rows]
    lots = jnp.where(jnp.arange(rows)[:, None] == holders[None, :], 1 << 14, lots)
    merit = lots * amount + jnp.arange(amount)
    return lax.top_k(merit.astype(jnp.int32), top)[1].astype(jnp.int32)


def noise(key, dims, width, limit, split=(), held_as=jnp.bfloat16):
    drawn = jax.random.normal(key, dims, jnp.float32) * width
    if len(split) > 0:
        drawn = steps_of(key, dims, split, -0.22, 0.18) * drawn
    return jnp.clip(drawn, min=-limit, max=limit).astype(held_as)


def setup_inputs(seed: int = 0) -> dict:
    key_of = jax.random.split(jax.random.key(seed), 5)
    points = noise(key_of[0], (NPB * BLK, D), 1.0, 6.0, ((0, 128),))
    candidates = noise(key_of[1], (NCB * BLK, D), D ** -0.5, 0.1875, ((0, 16),))
    probes = picks_of(key_of[2], NPB, NCB, PROBES, 4096)
    chosen = place_ends(jax.random.randint(key_of[3], (STEPS,), 0, NCB * BLK), jax.random.fold_in(key_of[3], 1), 0, (NCB * BLK) - 1).astype(jnp.int32)
    return {"points": points, "candidates": candidates, "probes": probes, "chosen": chosen}


def reference(points, candidates, probes, chosen):
    cand_count = candidates.shape[0] // BLK
    facility = jnp.take(candidates, chosen, axis=0)
    facility_sim = jnp.dot(points, facility.T, preferred_element_type=jnp.float32)
    covered = jnp.zeros((points.shape[0],), jnp.float32)
    columns = []
    for round_index in range(STEPS):
        columns.append(covered)
        covered = jnp.maximum(covered, facility_sim[:, round_index])
    before = jnp.stack(columns, axis=1)
    cand_blocks = candidates.reshape(cand_count, BLK, D)
    labels = jnp.arange(cand_count, dtype=jnp.int32)

    def add_block(running, inputs):
        point_rows, probe_row, before_rows = inputs
        picked = jnp.take(cand_blocks, probe_row, axis=0).reshape(PROBES * BLK, D)
        similar = jnp.dot(point_rows, picked.T, preferred_element_type=jnp.float32)
        contrib = jnp.maximum(similar[None, :, :] - before_rows.T[:, :, None], 0.0)
        summed = jnp.sum(contrib, axis=1).reshape(STEPS, PROBES, BLK)
        onehot = (probe_row[:, None] == labels[None, :]).astype(jnp.float32)
        added = jnp.einsum("spr,pc->scr", summed, onehot, precision=lax.Precision.HIGHEST)
        return running + added, None

    start_value = jnp.zeros((STEPS, cand_count, BLK), jnp.float32)

    def add_group(outer, inputs):
        inner, _ = lax.scan(add_block, jnp.zeros((STEPS, cand_count, BLK), jnp.float32), inputs)
        return outer + inner, None

    group_count = points.shape[0] // (BLK * PB_DEV)
    grouped = (points.reshape(group_count, PB_DEV, BLK, D), probes.reshape(group_count, PB_DEV, PROBES), before.reshape(group_count, PB_DEV, BLK, STEPS))
    running, _ = lax.scan(add_group, start_value, grouped)
    facility_gains = running.reshape(STEPS, cand_count * BLK) / (BLK * PROBES)
    return facility_gains, covered
```

```python
import functools

import jax
import jax.numpy as jnp
from jax import lax
from jax.experimental import pallas as pl
from jax.experimental.pallas import tpu as pltpu
from jax.sharding import PartitionSpec as P

BLK = 128
PROBES = 24
STEPS = 4
FEATURE = 1024
ROWS = 768
OWN = 1024
QUARTER = 192
PART = 96
HALF = 48
GROUP = 384
SUBS = 12
TILES = 32
FAR = -3e38
NT = (((1,), (1,)), ((), ()))
MESH = pl.DeviceIdType.MESH
A, B = 0, 1

ORDER = (
    (A, 1, 0), (A, 3, 0), (B, 1, 0), (B, 3, 0),
    (A, 0, 3), (A, 0, 1), (B, 0, 3), (B, 0, 1),
    (A, 0, 0), (B, 0, 0), (A, 2, 0), (B, 2, 0),
    (A, 1, 3), (A, 1, 1), (B, 1, 3), (B, 1, 1),
    (A, 3, 3), (A, 3, 1), (B, 3, 3), (B, 3, 1),
    (A, 2, 3), (A, 2, 1), (B, 2, 3), (B, 2, 1),
    (A, 0, 2), (B, 0, 2), (A, 1, 2), (B, 1, 2),
    (A, 3, 2), (B, 3, 2), (A, 2, 2), (B, 2, 2),
)
POS = {key: i for i, key in enumerate(ORDER)}


def tile_of(t):
    group = jnp.where(t < 6, t // 2, jnp.where(t < 9, t - 6, jnp.where(t < 15, 3 + (t - 9) // 3, jnp.where(t < 20, t - 15, 5 + (t - 20) // 4))))
    unit = jnp.where(t < 6, t % 2, jnp.where(t < 9, 2, jnp.where(t < 15, (t - 9) % 3, jnp.where(t < 20, 3, (t - 20) % 4))))
    return group, unit


def kernel(
    points, cands, probes, chosen, gains, cover,
    held, pts, shard, acc, pen, before, bsum, sim0, sim1, lists, fac, sent, got, both, ids,
    loc_sem, cand_s, cand_r, fac_s, fac_r, pt_s, pt_r, aux_s, aux_r, red_s, red_r, last_s, last_r,
):
    me = lax.axis_index("pts")
    y = lax.axis_index("ca")
    z = lax.axis_index("cb")
    x, core = me // 2, me % 2
    quarter = 2 * (x % 2) + core
    way = 1 - 2 * core

    def plane(dy, dz):
        return (me, (y + dy + 4) % 4, (z + dz + 4) % 4)

    sibling = (2 * x + 1 - core, y, z)
    beside = (2 * ((x + way + 4) % 4) + core, y, z)

    def along(part, du, dv):
        return plane(du, dv) if part == A else plane(dv, du)

    def cand_copy(part, du, dv, half=None):
        row, size = POS[part, du, dv] * PART, PART
        if half is not None:
            row, size = row + half * HALF, HALF
        if dv == 0:
            hop_u, hop_v = {1: -1, 3: 1, 2: (1 if half == 0 else -1)}[du], 0
            source = (part, 0, 0) if du != 2 else (part, 3 if half == 0 else 1, 0)
        else:
            hop_u, hop_v = 0, {1: -1, 3: 1, 2: (1 if half == 0 else -1)}[dv]
            source = (part, du, 0) if dv != 2 else (part, du, 3 if half == 0 else 1)
        if source[1:] == (0, 0):
            src = cands.at[pl.ds(quarter * QUARTER + part * PART, PART)]
        else:
            first = POS[source] * PART + (0 if half is None else half * HALF)
            src = held.at[pl.ds(first, size)]
        k = ((part * 4 + du) * 4 + dv) * 2 + (half or 0)
        return pltpu.make_async_remote_copy(
            src_ref=src, dst_ref=held.at[pl.ds(row, size)], send_sem=cand_s.at[k], recv_sem=cand_r.at[k],
            device_id=along(part, hop_u, hop_v), device_id_type=MESH)

    def fac_copy(dy, dz):
        k = ((4 - dy) % 4) * 4 + (4 - dz) % 4
        return pltpu.make_async_remote_copy(
            src_ref=fac.at[0], dst_ref=fac.at[k], send_sem=fac_s.at[k], recv_sem=fac_r.at[k],
            device_id=plane(dy, dz), device_id_type=MESH)

    def remote(src, dst, send, recv, k, device):
        return pltpu.make_async_remote_copy(src_ref=src, dst_ref=dst, send_sem=send.at[k], recv_sem=recv.at[k], device_id=device, device_id_type=MESH)

    def point_copy(kind):
        if kind == 0:
            return remote(points, pts.at[1], pt_s, pt_r, 0, sibling)
        unit = 2 + (kind - 1) % 2
        here = pts.at[unit, pl.ds(core * 512, 512)]
        if kind <= 2:
            return remote(points.at[pl.ds((unit - 2) * 512, 512)], here, pt_s, pt_r, kind, beside)
        return remote(here, here, pt_s, pt_r, kind, sibling)

    def point_landed(kind):
        unit = 2 + (kind - 1) % 2
        there = pts.at[unit, pl.ds((1 - core) * 512, 512)]
        return remote(there, there, pt_s, pt_r, kind, sibling)

    def list_copy(kind):
        if kind == 0:
            return remote(lists.at[0], lists.at[1], aux_s, aux_r, 0, sibling)
        if kind == 1:
            return remote(lists.at[0], lists.at[2 + core], aux_s, aux_r, 1, beside)
        return remote(lists.at[2 + core], lists.at[2 + core], aux_s, aux_r, 2, sibling)

    def before_copy(kind):
        if kind == 0:
            return remote(before.at[0], before.at[1], aux_s, aux_r, 3, sibling)
        unit = 2 + (kind - 1) % 2
        here = before.at[unit, :, pl.ds(core * 512, 512)]
        if kind <= 2:
            return remote(before.at[0, :, pl.ds((unit - 2) * 512, 512)], here, aux_s, aux_r, 3 + kind, beside)
        return remote(here, here, aux_s, aux_r, 3 + kind, sibling)

    def before_landed(kind):
        unit = 2 + (kind - 1) % 2
        there = before.at[unit, :, pl.ds((1 - core) * 512, 512)]
        return remote(there, there, aux_s, aux_r, 3 + kind, sibling)

    def gain_copy(part, du, dv):
        k = part * 16 + ((4 - du) % 4) * 4 + (4 - dv) % 4
        return remote(sent.at[POS[part, du, dv]], got.at[k], red_s, red_r, k, along(part, du, dv))

    def last_copy(k):
        return remote(both.at[me], both.at[me], last_s, last_r, k, ((me + k) % 8, y, z))

    own_points = pltpu.make_async_copy(points, pts.at[0], loc_sem.at[0])
    own_shard = pltpu.make_async_copy(cands, shard, loc_sem.at[1])
    own_parts = pltpu.make_async_copy(cands.at[pl.ds(quarter * QUARTER, QUARTER)], held.at[pl.ds(POS[A, 0, 0] * PART, QUARTER)], loc_sem.at[2])
    own_shard.start()
    own_points.start()
    own_parts.start()
    bar = pltpu.get_barrier_semaphore()
    others = [(dy, dz) for dy in range(4) for dz in range(4) if (dy, dz) != (0, 0)]
    for dy, dz in others:
        pl.semaphore_signal(bar, inc=1, device_id=plane(dy, dz), device_id_type=MESH)
    for k in range(1, 8):
        pl.semaphore_signal(bar, inc=1, device_id=((me + k) % 8, y, z), device_id_type=MESH)

    own_shard.wait()
    row = lax.broadcasted_iota(jnp.int32, (16, ROWS), 0)
    lane = lax.broadcasted_iota(jnp.int32, (16, ROWS), 1)
    pick = jnp.zeros((16, ROWS), jnp.float32)
    for s in range(STEPS):
        local_id = chosen[s] - (y * 4 + z) * ROWS
        pick = jnp.where((row % 4 == s) & (lane == local_id), 1.0, pick)
    mine = jnp.zeros((16, 256), jnp.float32)
    for j in range(4):
        pick_j = jnp.where(row // 4 == j, pick, 0.0).astype(jnp.bfloat16)
        mine = mine + jnp.dot(pick_j, shard[:, j * 256 : (j + 1) * 256], preferred_element_type=jnp.float32)
    fac[0] = mine.astype(jnp.bfloat16)
    lists[0] = jnp.full((8, 128), -1, jnp.int32)
    lists[0, :, 0:PROBES] = probes[...]

    pl.semaphore_wait(bar, 22)
    for dy, dz in others:
        fac_copy(dy, dz).start()
    for key in ((A, 1, 0), (A, 3, 0), (B, 1, 0), (B, 3, 0)):
        cand_copy(*key).start()
    list_copy(0).start()
    list_copy(1).start()
    point_copy(0).start()
    point_copy(1).start()
    for key in ((A, 0, 3), (A, 0, 1), (B, 0, 3), (B, 0, 1)):
        cand_copy(*key).start()

    for i, (part, du, dv) in enumerate(ORDER):
        at_y, at_z = (y + (du, dv)[part]) % 4, (z + (dv, du)[part]) % 4
        for r in range(3):
            ids[i * 3 + r] = (at_y * 4 + at_z) * 6 + (quarter * QUARTER + part * PART + r * 32) // BLK

    def build_pen(unit, listed):
        def one(i, _):
            hit = jnp.max(jnp.where(listed == ids[i], 1.0, 0.0), axis=1, keepdims=True)
            pen[unit, i] = jnp.broadcast_to(jnp.where(hit > 0.0, 0.0, FAR), (8, BLK))
            return 0

        lax.fori_loop(0, 96, one, 0, unroll=8)

    build_pen(0, lists[0])

    def zero(i, _):
        for s in range(STEPS):
            acc[s, pl.ds(i * 384, 384), :] = jnp.zeros((384, BLK), jnp.float32)
        return 0

    lax.fori_loop(0, 9, zero, 0)
    sent[...] = jnp.zeros_like(sent)

    for dy, dz in others:
        fac_copy(dy, dz).wait_recv()
    whole = fac[0].astype(jnp.float32)
    for k in range(1, 16):
        whole = whole + fac[k].astype(jnp.float32)
    wide = jnp.concatenate([whole if j == 0 else pltpu.roll(whole, 16 - 4 * j, 0) for j in range(4)], axis=1).astype(jnp.bfloat16)
    own_points.wait()
    facility_sim = lax.dot_general(wide, pts[0], NT, preferred_element_type=jnp.float32)
    before[0] = jnp.zeros((8, OWN), jnp.float32)
    covered = jnp.zeros((1, OWN), jnp.float32)
    for s in range(STEPS):
        covered = jnp.maximum(covered, facility_sim[s : s + 1, :])
        if s < STEPS - 1:
            before[0, s + 1 : s + 2, :] = covered
    cover[...] = covered
    for kind in (0, 1, 2):
        before_copy(kind).start()
    point_copy(2).start()

    list_copy(0).wait_recv()
    build_pen(1, lists[1])
    point_copy(0).wait_recv()
    before_copy(0).wait_recv()
    own_parts.wait()

    def finalize(group):
        ones = jnp.ones((8, 2 * BLK), jnp.bfloat16)
        for k in range(4):
            for s in range(STEPS):
                total = acc[s, pl.ds(pl.multiple_of(group * GROUP + k * PART, 32), PART), :] - bsum[s : s + 1, :]
                high = total.astype(jnp.bfloat16)
                low = (total - high.astype(jnp.float32)).astype(jnp.bfloat16)
                line = lax.dot_general(ones, jnp.concatenate([high, low], axis=1), NT, preferred_element_type=jnp.float32)
                sent[group * 4 + k, s : s + 1, 0:PART] = line[s : s + 1, :]

    def send_gains(group):
        for part, du, dv in ORDER[group * 4 : group * 4 + 4]:
            if (du, dv) == (0, 0):
                got[part * 16] = sent[POS[part, 0, 0]]
            else:
                gain_copy(part, du, dv).start()

    def at0():
        for key in ((A, 1, 0), (A, 3, 0), (B, 1, 0), (B, 3, 0)):
            cand_copy(*key).wait_recv()
        for part in (A, B):
            for half in (0, 1):
                cand_copy(part, 2, 0, half).start()
        for du in (1, 3):
            for part in (A, B):
                for dv in (3, 1):
                    cand_copy(part, du, dv).start()

    def at2():
        for key in ((A, 0, 3), (A, 0, 1), (B, 0, 3), (B, 0, 1)):
            cand_copy(*key).wait_recv()
        for part in (A, B):
            for half in (0, 1):
                cand_copy(part, 0, 2, half).start()
        list_copy(1).wait_recv()
        list_copy(2).start()
        for kind in (1, 2):
            before_copy(kind).wait_recv()
            before_copy(kind + 2).start()

    def at4():
        for part in (A, B):
            for half in (0, 1):
                cand_copy(part, 2, 0, half).wait_recv()
        for part in (A, B):
            for dv in (3, 1):
                cand_copy(part, 2, dv).start()
        remote(lists.at[3 - core], lists.at[3 - core], aux_s, aux_r, 2, sibling).wait_recv()
        for kind in (3, 4):
            before_landed(kind).wait_recv()
        build_pen(2, jnp.concatenate([lists[2, 0:4], lists[3, 0:4]], axis=0))
        build_pen(3, jnp.concatenate([lists[2, 4:8], lists[3, 4:8]], axis=0))
        total = jnp.zeros((8, BLK), jnp.float32)
        for unit in range(4):
            for j in range(8):
                total = total + before[unit, :, j * BLK : (j + 1) * BLK]
        bsum[...] = total

    def at5():
        point_copy(1).wait_recv()
        point_copy(3).start()

    def at6():
        point_landed(3).wait_recv()

    def s4(du):
        for part in (A, B):
            for dv in (3, 1):
                cand_copy(part, du, dv).wait_recv()
        for part in (A, B):
            for half in (0, 1):
                cand_copy(part, du, 2, half).start()

    def at14():
        point_copy(2).wait_recv()
        point_copy(4).start()

    def at15():
        point_landed(4).wait_recv()

    def halves_landed(*dus):
        for du in dus:
            for part in (A, B):
                for half in (0, 1):
                    cand_copy(part, du, 2, half).wait_recv()

    events = {
        0: at0, 2: at2, 4: at4, 5: at5, 6: at6, 9: lambda: s4(1), 12: lambda: s4(3), 14: at14, 15: at15,
        18: lambda: s4(2), 24: lambda: halves_landed(0, 1), 28: lambda: halves_landed(3, 2),
    }
    done = {17: 0, 18: 1, 19: 2, 20: 3, 21: 4, 25: 5, 29: 6}

    def prepare(t, parity):
        for when, event in events.items():
            if when % 2 == parity:
                pl.when(t == when)(event)
        ready = ((t >= 17) & (t <= 21)) | (t == 25) | (t == 29)
        pl.when(ready)(lambda: finalize(jnp.where(t <= 21, t - 17, jnp.where(t == 25, 5, 6))))
        for when, group in done.items():
            if when % 2 == parity:
                pl.when(t == when)(functools.partial(send_gains, group))

    def product(t, sim):
        group, unit = tile_of(t)
        sim[...] = lax.dot_general(held[pl.ds(pl.multiple_of(group * GROUP, GROUP), GROUP), :], pts[unit], NT, preferred_element_type=jnp.float32)

    def hinge(t, sim):
        group, unit = tile_of(t)
        group = jnp.where(t < 0, 8, group)
        unit = jnp.where(t < 0, 0, unit)
        slot = jnp.where(t < 0, 0, group)
        for r in range(SUBS):
            rows = pl.ds(pl.multiple_of(group * GROUP + r * 32, 32), 32)
            sums = [acc[s, rows, :] for s in range(STEPS)]
            for j in range(8):
                cols = slice(j * BLK, (j + 1) * BLK)
                value = sim[r * 32 : (r + 1) * 32, cols] + pen[unit, slot * SUBS + r, j : j + 1, :]
                sums[0] = sums[0] + jnp.maximum(value, 0.0)
                for s in range(1, STEPS):
                    sums[s] = sums[s] + jnp.maximum(value, before[unit, s : s + 1, cols])
            for s in range(STEPS):
                acc[s, rows, :] = sums[s]

    sim1[...] = jnp.zeros_like(sim1)

    def pair(i, _):
        t = i * 2
        prepare(t, 0)
        product(t, sim0)
        hinge(t - 1, sim1)
        prepare(t + 1, 1)
        product(t + 1, sim1)
        hinge(t, sim0)
        return 0

    lax.fori_loop(0, TILES // 2, pair, 0)
    hinge(jnp.int32(TILES - 1), sim1)
    finalize(jnp.int32(7))
    send_gains(7)

    for part, du, dv in ORDER:
        if (du, dv) != (0, 0):
            gain_copy(part, du, dv).wait_recv()
    for part in (A, B):
        total = got[part * 16]
        for k in range(1, 16):
            total = total + got[part * 16 + k]
        both[me, part] = total
    for k in range(1, 8):
        last_copy(k).start()
    for k in range(1, 8):
        source = both.at[(me + 8 - k) % 8]
        remote(source, source, last_s, last_r, k, ((me + k) % 8, y, z)).wait_recv()
    for q in range(4):
        gains[q] = (both[q] + both[q + 4]) / (BLK * PROBES)

    for part, du, dv in ORDER:
        if (du, dv) != (0, 0):
            gain_copy(part, du, dv).wait_send()
            for half in (0, 1) if 2 in (du, dv) and not (du == 2 and dv in (1, 3)) else (None,):
                cand_copy(part, du, dv, half).wait_send()
    for dy, dz in others:
        fac_copy(dy, dz).wait_send()
    for kind in range(5):
        point_copy(kind).wait_send()
        before_copy(kind).wait_send()
    for kind in range(3):
        list_copy(kind).wait_send()
    for k in range(1, 8):
        last_copy(k).wait_send()


def local(points, candidates, probes, chosen):
    any_spec = pl.BlockSpec(memory_space=pl.ANY)
    vmem = pl.BlockSpec(memory_space=pltpu.VMEM)
    f32, bf16 = jnp.float32, jnp.bfloat16
    dma = pltpu.SemaphoreType.DMA
    gains, cover = pl.pallas_call(
        kernel,
        out_shape=(jax.ShapeDtypeStruct((4, 2, 8, BLK), f32), jax.ShapeDtypeStruct((1, OWN), f32)),
        in_specs=[any_spec, any_spec, vmem, pl.BlockSpec(memory_space=pltpu.SMEM)],
        out_specs=(vmem, vmem),
        scratch_shapes=[
            pltpu.VMEM((32 * PART, FEATURE), bf16),
            pltpu.VMEM((4, OWN, FEATURE), bf16),
            pltpu.VMEM((ROWS, FEATURE), bf16),
            pltpu.VMEM((STEPS, 9 * GROUP, BLK), f32),
            pltpu.VMEM((4, 96, 8, BLK), f32),
            pltpu.VMEM((4, 8, OWN), f32),
            pltpu.VMEM((8, BLK), f32),
            pltpu.VMEM((GROUP, OWN), f32),
            pltpu.VMEM((GROUP, OWN), f32),
            pltpu.VMEM((4, 8, BLK), jnp.int32),
            pltpu.VMEM((16, 16, 256), bf16),
            pltpu.VMEM((32, 8, BLK), f32),
            pltpu.VMEM((32, 8, BLK), f32),
            pltpu.VMEM((8, 2, 8, BLK), f32),
            pltpu.SMEM((96,), jnp.int32),
            dma((3,)),
            dma((64,)), dma((64,)),
            dma((16,)), dma((16,)),
            dma((5,)), dma((5,)),
            dma((8,)), dma((8,)),
            dma((32,)), dma((32,)),
            dma((8,)), dma((8,)),
        ],
        compiler_params=pltpu.CompilerParams(collective_id=0, has_side_effects=True, vmem_limit_bytes=50 << 20),
        name="gather_gain",
    )(points, candidates, probes, chosen)
    gains = gains[:, :, :STEPS, :PART].transpose(2, 0, 1, 3).reshape(STEPS, ROWS)
    return (gains, cover.reshape(OWN))


def solution(mesh):
    return jax.shard_map(
        local,
        mesh=mesh,
        in_specs=(P(("pts", "ca", "cb"), None), P(("ca", "cb"), None), P(("pts", "ca", "cb"), None), P()),
        out_specs=(P(None, ("ca", "cb")), P(("pts", "ca", "cb"))),
        check_vma=False,
    )
```

```python
import functools

import jax
import jax.numpy as jnp
from jax import lax
from jax.experimental import pallas as pl
from jax.experimental.pallas import tpu as pltpu
from jax.sharding import PartitionSpec as P

BLK = 128
PROBES = 24
STEPS = 4
FEATURE = 1024
ROWS = 768
OWN = 1024
QUARTER = 192
PART = 96
HALF = 48
GROUP = 768
UNIT = 512
CHUNK = 256
BLOCKS = 16
NT = (((1,), (1,)), ((), ()))
MESH = pl.DeviceIdType.MESH
A, B = 0, 1


def halves(*keys):
    return [(part, du, dv, h) for part, du, dv in keys for h in (0, 1)]


def ring(du, dvs, hs):
    return [(part, du, dv, h) for part in (A, B) for dv in dvs for h in hs]


FIRST = halves((A, 1, 0), (A, 3, 0), (B, 1, 0), (B, 3, 0))
OPPOSITE = halves((A, 2, 0), (B, 2, 0))
ORDER = (
    halves((A, 0, 0), (B, 0, 0)) + FIRST + ring(0, (3, 1), (0,))
    + ring(0, (3, 1), (1,)) + OPPOSITE + ring(1, (3, 1), (0,)) + ring(1, (3, 1), (1,))
    + ring(3, (3, 1), (0, 1)) + ring(0, (2,), (0, 1)) + ring(2, (3, 1), (0,))
    + ring(2, (3, 1), (1,)) + ring(1, (2,), (0, 1)) + ring(3, (2,), (0, 1)) + ring(2, (2,), (0, 1))
)
POS = {key: i for i, key in enumerate(ORDER)}
WAVES = (
    FIRST, ring(0, (3, 1), (0,)), ring(0, (3, 1), (1,)) + OPPOSITE + ring(1, (3, 1), (0,)), ring(1, (3, 1), (1,)),
    ring(3, (3, 1), (0, 1)) + ring(0, (2,), (0, 1)) + ring(2, (3, 1), (0,)), ring(2, (3, 1), (1,)),
    ring(1, (2,), (0, 1)) + ring(3, (2,), (0, 1)) + ring(2, (2,), (0, 1)),
)
WAVE = {key: i for i, wave in enumerate(WAVES) for key in wave}


def tile_of(t):
    pick = jnp.where
    group = pick(t < 6, 0, pick(t < 12, 1, pick(t < 14, t - 12, pick(t < 22, 2, pick(t < 24, t - 22, 3)))))
    unit = pick(t < 6, t, pick(t < 12, t - 6, pick(t < 14, 6, pick(t < 22, t - 14, pick(t < 24, 7, t - 24)))))
    return group, unit


def kernel(
    points, cands, listed_own, gains, cover,
    held, pts, shard, acc, mask, before, bsum, fsim, sim0, sim1, lists, ids, fac, repeated, sent, got, both,
    loc_sem, cand_s, cand_r, fac_s, fac_r, pt_s, pt_r, aux_s, aux_r, red_s, red_r, last_s, last_r,
):
    me = lax.axis_index("pts")
    y = lax.axis_index("ca")
    z = lax.axis_index("cb")
    x, core = me // 2, me % 2
    quarter = 2 * (x % 2) + core
    way = 1 - 2 * core

    def plane(dy, dz):
        return (me, (y + dy + 4) % 4, (z + dz + 4) % 4)

    sibling = (2 * x + 1 - core, y, z)
    beside = (2 * ((x + way + 4) % 4) + core, y, z)

    def along(part, du, dv):
        return plane(du, dv) if part == A else plane(dv, du)

    def remote(src, dst, send, recv, device, k=0):
        return pltpu.make_async_remote_copy(src_ref=src, dst_ref=dst, send_sem=send.at[0], recv_sem=recv.at[k], device_id=device, device_id_type=MESH)

    def cand_copy(part, du, dv, half):
        row = POS[part, du, dv, half] * HALF
        if dv == 0:
            hop_u, hop_v = {1: -1, 3: 1, 2: (1 if half == 0 else -1)}[du], 0
            source = (part, 0, 0) if du != 2 else (part, 3 if half == 0 else 1, 0)
        else:
            hop_u, hop_v = 0, {1: -1, 3: 1, 2: (1 if half == 0 else -1)}[dv]
            source = (part, du, 0) if dv != 2 else (part, du, 3 if half == 0 else 1)
        if source[1:] == (0, 0):
            src = cands.at[pl.ds(quarter * QUARTER + part * PART + half * HALF, HALF)]
        else:
            src = held.at[pl.ds(POS[source + (half,)] * HALF, HALF)]
        return remote(src, held.at[pl.ds(row, HALF)], cand_s, cand_r, along(part, hop_u, hop_v), WAVE[part, du, dv, half])

    def go(keys):
        for key in keys:
            cand_copy(*key).start()

    def landed(wave):
        at = [i for i, key in enumerate(ORDER) if WAVE.get(key) == wave]
        rows = held.at[pl.ds(at[0] * HALF, len(at) * HALF)]
        remote(rows, rows, cand_s, cand_r, sibling, wave).wait_recv()

    def fac_copy(dy, dz):
        k = ((4 - dy) % 4) * 4 + (4 - dz) % 4
        return remote(fac.at[0], fac.at[k], fac_s, fac_r, plane(dy, dz))

    def own_copy(i):
        return remote(points.at[pl.ds(i * UNIT, UNIT)], pts.at[pl.ds((2 + i) * UNIT, UNIT)], pt_s, pt_r, sibling)

    def chunk_at(i, side):
        return pts.at[pl.ds((4 + i) * UNIT + side * CHUNK, CHUNK)]

    def beside_copy(i):
        return remote(points.at[pl.ds(i * CHUNK, CHUNK)], chunk_at(i, core), pt_s, pt_r, beside, 1 + i)

    def pass_copy(i, side):
        return remote(chunk_at(i, side), chunk_at(i, side), pt_s, pt_r, sibling, 5 + i)

    def list_copy(kind, side):
        if kind == 0:
            return remote(lists.at[0], lists.at[1], aux_s, aux_r, sibling)
        if kind == 1:
            return remote(lists.at[0], lists.at[2 + side], aux_s, aux_r, beside, 1)
        return remote(lists.at[2 + side], lists.at[2 + side], aux_s, aux_r, sibling, 2)

    def gain_copy(part, du, dv):
        k = part * 16 + ((4 - du) % 4) * 4 + (4 - dv) % 4
        return remote(sent.at[(part * 4 + du) * 4 + dv], got.at[k], red_s, red_r, along(part, du, dv))

    def last_copy(k, slot):
        return remote(both.at[slot], both.at[slot], last_s, last_r, ((me + k) % 8, y, z))

    bar = pltpu.get_barrier_semaphore()
    others = [(dy, dz) for dy in range(4) for dz in range(4) if (dy, dz) != (0, 0)]
    for dy, dz in others:
        pl.semaphore_signal(bar, inc=1, device_id=plane(dy, dz), device_id_type=MESH)
    for k in range(1, 8):
        pl.semaphore_signal(bar, inc=1, device_id=((me + k) % 8, y, z), device_id_type=MESH)
    local_copies = [
        pltpu.make_async_copy(cands, shard, loc_sem.at[0]),
        pltpu.make_async_copy(cands.at[pl.ds(quarter * QUARTER, QUARTER)], held.at[pl.ds(0, QUARTER)], loc_sem.at[1]),
        pltpu.make_async_copy(points, pts.at[pl.ds(0, OWN)], loc_sem.at[2]),
    ]
    for copy in local_copies:
        copy.start()
    sent[...] = jnp.zeros_like(sent)
    got[0] = jnp.zeros((8, BLK), jnp.float32)
    got[16] = jnp.zeros((8, BLK), jnp.float32)
    acc[...] = jnp.zeros_like(acc)
    sim1[...] = jnp.zeros_like(sim1)
    lists[0] = listed_own[...]

    local_copies[0].wait()
    row = lax.broadcasted_iota(jnp.int32, (16, ROWS), 0)
    lane = lax.broadcasted_iota(jnp.int32, (16, ROWS), 1)
    pick = jnp.zeros((16, ROWS), jnp.float32)
    for s in range(STEPS):
        wanted = lists[0, :, PROBES + s : PROBES + s + 1] - (y * 4 + z) * ROWS
        pick = jnp.where((row % 4 == s) & (lane == jnp.concatenate([wanted, wanted], axis=0)), 1.0, pick)
    mine = jnp.zeros((16, 256), jnp.float32)
    for j in range(4):
        pick_j = jnp.where(row // 4 == j, pick, 0.0).astype(jnp.bfloat16)
        mine = mine + jnp.dot(pick_j, shard[:, j * 256 : (j + 1) * 256], preferred_element_type=jnp.float32)
    fac[0] = mine.astype(jnp.bfloat16)

    pl.semaphore_wait(bar, 22)
    for dy, dz in others:
        fac_copy(dy, dz).start()
    list_copy(1, core).start()
    list_copy(0, core).start()
    go(key for key in FIRST if key[3] == 0)
    go(key for key in FIRST if key[3] == 1)
    go(ring(0, (3, 1), (0,)))
    go(ring(0, (3, 1), (1,)))
    for i in range(4):
        beside_copy(i).start()
    own_copy(0).start()
    own_copy(1).start()

    lane = lax.broadcasted_iota(jnp.int32, (8, GROUP), 1)
    for g in range(4):
        base = jnp.zeros((8, GROUP), jnp.int32)
        for i, (part, du, dv, h) in enumerate(ORDER[g * 16 : g * 16 + 16]):
            at_y, at_z = (y + (du, dv)[part]) % 4, (z + (dv, du)[part]) % 4
            begin = (at_y * 4 + at_z) * ROWS + quarter * QUARTER + part * PART + (h - i) * HALF
            base = jnp.where(lane >= i * HALF, begin, base)
        ids[g] = lax.shift_right_logical(base + lane, 7)

    def build_mask(unit, listed):
        for g in range(4):
            hit = ids[g] == listed[:, 0:1]
            for k in range(1, PROBES):
                hit = hit | (ids[g] == listed[:, k : k + 1])
            hit = jnp.where(hit, 1.0, 0.0)
            mask[unit, g, 0:4, :] = hit[0:4]
            mask[unit + 1, g, 0:4, :] = hit[4:8]

    build_mask(0, lists[0])
    list_copy(0, core).wait_recv()
    build_mask(2, lists[1])
    list_copy(1, core).wait_recv()
    list_copy(2, core).start()

    slots = fac.at[pl.ds(1, 15)]
    remote(slots, slots, fac_s, fac_r, sibling).wait_recv()
    whole = fac[0].astype(jnp.float32)
    for k in range(1, 16):
        whole = whole + fac[k].astype(jnp.float32)
    wide = jnp.concatenate([whole if j == 0 else pltpu.roll(whole, 16 - 4 * j, 0) for j in range(4)], axis=1).astype(jnp.bfloat16)
    for s in range(3):
        repeated[s * BLK : (s + 1) * BLK, :] = jnp.broadcast_to(wide[s : s + 1, :], (BLK, FEATURE))
    repeated[3 * BLK : 3 * BLK + 16, :] = wide

    def thresholds(unit):
        rows = pl.ds(unit * UNIT, UNIT)
        if not isinstance(unit, int):
            rows = pl.ds(pl.multiple_of(unit * UNIT, UNIT), UNIT)
        fsim[...] = lax.dot_general(pts[rows, :], repeated[0 : 3 * BLK, :], NT, preferred_element_type=jnp.float32)
        for q in range(4):
            sums = [jnp.zeros((8, BLK), jnp.float32) for _ in range(3)]
            for r in range(16):
                at = slice(q * BLK + r * 8, q * BLK + r * 8 + 8)
                covered = jnp.zeros((8, BLK), jnp.float32)
                for s in range(3):
                    covered = jnp.maximum(covered, fsim[at, s * BLK : (s + 1) * BLK])
                    before[unit, s, at, :] = covered
                    sums[s] = sums[s] + covered
            for s in range(3):
                bsum[unit, q, s] = sums[s]

    for copy in local_copies[1:]:
        copy.wait()
    lax.fori_loop(0, 2, lambda u, _: thresholds(u) or 0, 0)
    all_own = pts.at[pl.ds(2 * UNIT, OWN)]
    remote(all_own, all_own, pt_s, pt_r, sibling).wait_recv()
    lax.fori_loop(2, 4, lambda u, _: thresholds(u) or 0, 0)

    list_copy(2, 1 - core).wait_recv()
    left, right = lists[2], lists[3]
    build_mask(4, jnp.concatenate([left[0:2], right[0:2], left[2:4], right[2:4]], axis=0))
    build_mask(6, jnp.concatenate([left[4:6], right[4:6], left[6:8], right[6:8]], axis=0))
    landed(0)

    def send_gains(keys):
        totals = {}
        for part, du, dv in keys:
            pieces = []
            for h in (0, 1):
                g, i = divmod(POS[part, du, dv, h], 16)
                if g not in totals:
                    totals[g] = jnp.sum(acc[g], axis=1)
                pieces.append(totals[g][:, i * HALF : (i + 1) * HALF])
            slot = (part * 4 + du) * 4 + dv
            line = jnp.concatenate(pieces, axis=1)
            if (du, dv) == (0, 0):
                got[part * 16, 0:STEPS, 0:PART] = line
            else:
                sent[slot, 0:STEPS, 0:PART] = line
                gain_copy(part, du, dv).start()

    def coverage():
        facility_sim = lax.dot_general(repeated[3 * BLK : 3 * BLK + 16, :], pts[0:OWN, :], NT, preferred_element_type=jnp.float32)
        covered = jnp.zeros((1, OWN), jnp.float32)
        for s in range(STEPS):
            covered = jnp.maximum(covered, facility_sim[s : s + 1, :])
        cover[...] = covered

    def e0():
        landed(1)
        go(OPPOSITE)
        for du in (1, 3):
            for h in (0, 1):
                go(ring(du, (3, 1), (h,)))
        beside_copy(0).wait_recv()
        pass_copy(0, core).start()

    def e2():
        pass_copy(0, 1 - core).wait_recv()
        thresholds(4)
        beside_copy(1).wait_recv()
        pass_copy(1, core).start()
        coverage()
        pass_copy(1, 1 - core).wait_recv()
        thresholds(5)

    def e3():
        landed(2)
        go(ring(0, (2,), (0, 1)))
        go(ring(2, (3, 1), (0,)))
        go(ring(2, (3, 1), (1,)))
        landed(3)
        go(ring(1, (2,), (0, 1)))

    def e5():
        beside_copy(2).wait_recv()
        pass_copy(2, core).start()

    def e6():
        pass_copy(2, 1 - core).wait_recv()
        thresholds(6)

    def e7():
        landed(4)
        go(ring(3, (2,), (0, 1)))

    def e8():
        landed(5)
        go(ring(2, (2,), (0, 1)))

    def e9():
        beside_copy(3).wait_recv()
        pass_copy(3, core).start()

    def e10():
        pass_copy(3, 1 - core).wait_recv()
        thresholds(7)

    def e12():
        landed(6)
        send_gains([(p, 3, dv) for p in (A, B) for dv in (3, 1)] + [(p, 0, 2) for p in (A, B)])

    def e13():
        send_gains([(p, du, 0) for p in (A, B) for du in (0, 1, 3, 2)] + [(p, du, dv) for p in (A, B) for du in (0, 1) for dv in (3, 1)])

    events = {0: e0, 2: e2, 3: e3, 5: e5, 6: e6, 7: e7, 8: e8, 9: e9, 10: e10, 12: e12, 13: e13}

    def prepare(i, low, high):
        if high - low == 1:
            if low in events:
                events[low]()
            return
        middle = (low + high) // 2
        pl.when(i < middle)(functools.partial(prepare, i, low, middle))
        pl.when(i >= middle)(functools.partial(prepare, i, middle, high))

    def product(t, sim):
        group, unit = tile_of(t)
        sim[...] = lax.dot_general(
            pts[pl.ds(pl.multiple_of(unit * UNIT, UNIT), UNIT), :], held[pl.ds(pl.multiple_of(group * GROUP, GROUP), GROUP), :],
            NT, preferred_element_type=jnp.float32)

    def hinge(t, sim):
        group, unit = tile_of(t)
        unit = jnp.where(t < 0, 0, unit)
        slot = jnp.where(t < 0, 4, group)
        for q in range(4):
            sums = [[None] * 6 for _ in range(STEPS)]
            for r in range(16):
                rows = slice(q * BLK + r * 8, q * BLK + r * 8 + 8)
                floors = [before[unit, s, rows, :] for s in range(3)]
                for c in range(6):
                    value = sim[rows, c * BLK : (c + 1) * BLK]
                    tops = [jnp.maximum(value, 0.0)] + [jnp.maximum(value, floor) for floor in floors]
                    for s in range(STEPS):
                        sums[s][c] = tops[s] if r == 0 else sums[s][c] + tops[s]
            for c in range(6):
                cols = slice(c * BLK, (c + 1) * BLK)
                listed = mask[unit, group, q : q + 1, cols]
                for s in range(STEPS):
                    part = sums[s][c] if s == 0 else sums[s][c] - bsum[unit, q, s - 1]
                    acc[slot, s, :, cols] += part * listed

    def pair(i, _):
        t = i * 2
        prepare(i, 0, BLOCKS)
        product(t, sim0)
        hinge(t - 1, sim1)
        product(t + 1, sim1)
        hinge(t, sim0)
        return 0

    lax.fori_loop(0, BLOCKS, pair, 0)
    hinge(jnp.int32(2 * BLOCKS - 1), sim1)
    send_gains([(p, 2, dv) for p in (A, B) for dv in (3, 1)] + [(p, du, 2) for p in (A, B) for du in (1, 3, 2)])

    arrived = got.at[pl.ds(0, 30)]
    remote(arrived, arrived, red_s, red_r, sibling).wait_recv()
    for part in (A, B):
        total = got[part * 16]
        for k in range(1, 16):
            total = total + got[part * 16 + k]
        both[me, part] = total
    for k in range(1, 8):
        last_copy(k, me).start()
    seven = both.at[pl.ds(0, 7)]
    remote(seven, seven, last_s, last_r, sibling).wait_recv()
    for q in range(4):
        for part in (A, B):
            gains[q, part] = (both[q, part] + both[q + 4, part]) / (BLK * PROBES)

    for ref, send, recv in (
        (held.at[pl.ds(0, 60 * HALF)], cand_s, cand_r),
        (pts.at[pl.ds(0, 3 * OWN)], pt_s, pt_r),
        (slots, fac_s, fac_r),
        (lists.at[pl.ds(0, 3)], aux_s, aux_r),
        (arrived, red_s, red_r),
        (seven, last_s, last_r),
    ):
        remote(ref, ref, send, recv, sibling).wait_send()


def local(points, candidates, probes, chosen):
    hbm, vmem = pl.BlockSpec(memory_space=pltpu.HBM), pl.BlockSpec(memory_space=pltpu.VMEM)
    f32, bf16, i32 = jnp.float32, jnp.bfloat16, jnp.int32
    dma = pltpu.SemaphoreType.DMA
    listed = jnp.pad(probes, ((0, 0), (0, BLK - PROBES))) + jnp.pad(chosen, (PROBES, BLK - PROBES - STEPS))[None, :]
    gains, cover = pl.pallas_call(
        kernel,
        out_shape=(jax.ShapeDtypeStruct((4, 2, 8, BLK), f32), jax.ShapeDtypeStruct((1, OWN), f32)),
        in_specs=[hbm, hbm, vmem],
        out_specs=(vmem, vmem),
        scratch_shapes=[
            pltpu.VMEM((4 * GROUP, FEATURE), bf16),
            pltpu.VMEM((8 * UNIT, FEATURE), bf16),
            pltpu.VMEM((ROWS, FEATURE), bf16),
            pltpu.VMEM((5, STEPS, 8, GROUP), f32),
            pltpu.VMEM((8, 4, 8, GROUP), f32),
            pltpu.VMEM((8, 3, UNIT, BLK), f32),
            pltpu.VMEM((8, 4, 3, 8, BLK), f32),
            pltpu.VMEM((UNIT, 3 * BLK), f32),
            pltpu.VMEM((UNIT, GROUP), f32),
            pltpu.VMEM((UNIT, GROUP), f32),
            pltpu.VMEM((4, 8, BLK), i32),
            pltpu.VMEM((4, 8, GROUP), i32),
            pltpu.VMEM((16, 16, 256), bf16),
            pltpu.VMEM((3 * BLK + 16, FEATURE), bf16),
            pltpu.VMEM((32, 8, BLK), f32),
            pltpu.VMEM((32, 8, BLK), f32),
            pltpu.VMEM((8, 2, 8, BLK), f32),
            dma((3,)),
            dma((1,)), dma((7,)),
            dma((1,)), dma((1,)),
            dma((1,)), dma((9,)),
            dma((1,)), dma((3,)),
            dma((1,)), dma((1,)),
            dma((1,)), dma((1,)),
        ],
        compiler_params=pltpu.CompilerParams(collective_id=0, has_side_effects=True, vmem_limit_bytes=53 << 20),
        name="gather_gain",
    )(points, candidates, listed)
    gains = gains[:, :, :STEPS, :PART].transpose(2, 0, 1, 3).reshape(STEPS, ROWS)
    return (gains, cover.reshape(OWN))


def solution(mesh):
    return jax.shard_map(
        local,
        mesh=mesh,
        in_specs=(P(("pts", "ca", "cb"), None), P(("ca", "cb"), None), P(("pts", "ca", "cb"), None), P()),
        out_specs=(P(None, ("ca", "cb")), P(("pts", "ca", "cb"))),
        check_vma=False,
    )
```

```python
import functools

import jax
import jax.numpy as jnp
from jax import lax
from jax.experimental import pallas as pl
from jax.experimental.pallas import tpu as pltpu
from jax.sharding import PartitionSpec as P

BLK = 128
PROBES = 24
STEPS = 4
FEATURE = 1024
ROWS = 768
OWN = 1024
QUARTER = 192
PART = 96
HALF = 48
GROUP = 768
UNIT = 512
CHUNK = 256
BLOCKS = 16
NT = (((1,), (1,)), ((), ()))
MESH = pl.DeviceIdType.MESH
A, B = 0, 1


def halves(*keys):
    return [(part, du, dv, h) for part, du, dv in keys for h in (0, 1)]


def ring(du, dvs, hs):
    return [(part, du, dv, h) for part in (A, B) for dv in dvs for h in hs]


FIRST = halves((A, 1, 0), (A, 3, 0), (B, 1, 0), (B, 3, 0))
OPPOSITE = halves((A, 2, 0), (B, 2, 0))
ORDER = (
    halves((A, 0, 0), (B, 0, 0)) + FIRST + ring(0, (3, 1), (0,))
    + ring(0, (3, 1), (1,)) + OPPOSITE + ring(1, (3, 1), (0, 1))
    + ring(3, (3, 1), (0, 1)) + ring(0, (2,), (0, 1)) + ring(2, (3, 1), (0,))
    + ring(2, (3, 1), (1,)) + ring(1, (2,), (0, 1)) + ring(3, (2,), (0, 1)) + ring(2, (2,), (0, 1))
)
POS = {key: i for i, key in enumerate(ORDER)}
WAVES = (
    FIRST, ring(0, (3, 1), (0,)), ring(0, (3, 1), (1,)) + OPPOSITE, ring(1, (3, 1), (0, 1)),
    ring(3, (3, 1), (0, 1)), ring(0, (2,), (0, 1)) + ring(2, (3, 1), (0,)), ring(2, (3, 1), (1,)),
    ring(1, (2,), (0, 1)) + ring(3, (2,), (0, 1)) + ring(2, (2,), (0, 1)),
)
WAVE = {key: i for i, wave in enumerate(WAVES) for key in wave}


def tile_of(t):
    pick = jnp.where
    group = pick(t < 6, 0, pick(t < 12, 1, pick(t < 14, t - 12, pick(t < 22, 2, pick(t < 24, t - 22, 3)))))
    unit = pick(t < 6, t, pick(t < 12, t - 6, pick(t < 14, 6, pick(t < 22, t - 14, pick(t < 24, 7, t - 24)))))
    return group, unit


def kernel(
    points, cands, listed_own, gains, cover,
    held, pts, shard, acc, mask, before, fsim, sim0, sim1, lists, ids, fac, columns, repeated, sent, got, both,
    loc_sem, cand_s, cand_r, fac_s, fac_r, col_s, col_r, pt_s, pt_r, aux_s, aux_r, thr_s, thr_r, red_s, red_r, last_s, last_r,
):
    me = lax.axis_index("pts")
    y = lax.axis_index("ca")
    z = lax.axis_index("cb")
    x, core = me // 2, me % 2
    quarter = 2 * (x % 2) + core
    way = 1 - 2 * core

    def plane(dy, dz):
        return (me, (y + dy + 4) % 4, (z + dz + 4) % 4)

    sibling = (2 * x + 1 - core, y, z)
    beside = (2 * ((x + way + 4) % 4) + core, y, z)

    def along(part, du, dv):
        return plane(du, dv) if part == A else plane(dv, du)

    def remote(src, dst, send, recv, device, k=0):
        return pltpu.make_async_remote_copy(src_ref=src, dst_ref=dst, send_sem=send.at[0], recv_sem=recv.at[k], device_id=device, device_id_type=MESH)

    def cand_copy(part, du, dv, half):
        row = POS[part, du, dv, half] * HALF
        if dv == 0:
            hop_u, hop_v = {1: -1, 3: 1, 2: (1 if half == 0 else -1)}[du], 0
            source = (part, 0, 0) if du != 2 else (part, 3 if half == 0 else 1, 0)
        else:
            hop_u, hop_v = 0, {1: -1, 3: 1, 2: (1 if half == 0 else -1)}[dv]
            source = (part, du, 0) if dv != 2 else (part, du, 3 if half == 0 else 1)
        if source[1:] == (0, 0):
            src = cands.at[pl.ds(quarter * QUARTER + part * PART + half * HALF, HALF)]
        else:
            src = held.at[pl.ds(POS[source + (half,)] * HALF, HALF)]
        return remote(src, held.at[pl.ds(row, HALF)], cand_s, cand_r, along(part, hop_u, hop_v), WAVE[part, du, dv, half])

    def go(keys):
        for key in keys:
            cand_copy(*key).start()

    def landed(wave):
        at = [i for i, key in enumerate(ORDER) if WAVE.get(key) == wave]
        rows = held.at[pl.ds(at[0] * HALF, len(at) * HALF)]
        remote(rows, rows, cand_s, cand_r, sibling, wave).wait_recv()

    def fac_copy(dy, dz):
        k = ((4 - dy) % 4) * 4 + (4 - dz) % 4
        return remote(fac.at[0], fac.at[k], fac_s, fac_r, plane(dy, dz))

    def column_copy(side):
        return remote(columns.at[side], columns.at[side], col_s, col_r, sibling)

    def own_copy(i):
        return remote(points.at[pl.ds(i * UNIT, UNIT)], pts.at[pl.ds((2 + i) * UNIT, UNIT)], pt_s, pt_r, sibling)

    def chunk_at(i, side):
        return pts.at[pl.ds((4 + i) * UNIT + side * CHUNK, CHUNK)]

    def beside_copy(i):
        return remote(points.at[pl.ds(i * CHUNK, CHUNK)], chunk_at(i, core), pt_s, pt_r, beside, 1 + i)

    def pass_copy(i, side):
        return remote(chunk_at(i, side), chunk_at(i, side), pt_s, pt_r, sibling, 5 + i)

    def list_copy(kind, side):
        if kind == 0:
            return remote(lists.at[0], lists.at[1], aux_s, aux_r, sibling)
        if kind == 1:
            return remote(lists.at[0], lists.at[2 + side], aux_s, aux_r, beside, 1)
        return remote(lists.at[2 + side], lists.at[2 + side], aux_s, aux_r, sibling, 2)

    def own_before_copy(unit):
        return remote(before.at[unit], before.at[2 + unit], thr_s, thr_r, sibling)

    def before_copy(i, side):
        here = before.at[4 + i, :, side]
        return remote(here, here, thr_s, thr_r, sibling, 1 + i)

    def gain_copy(part, du, dv):
        k = part * 16 + ((4 - du) % 4) * 4 + (4 - dv) % 4
        return remote(sent.at[(part * 4 + du) * 4 + dv], got.at[k], red_s, red_r, along(part, du, dv))

    def last_copy(k, slot):
        return remote(both.at[slot], both.at[slot], last_s, last_r, ((me + k) % 8, y, z))

    bar = pltpu.get_barrier_semaphore()
    others = [(dy, dz) for dy in range(4) for dz in range(4) if (dy, dz) != (0, 0)]
    for dy, dz in others:
        pl.semaphore_signal(bar, inc=1, device_id=plane(dy, dz), device_id_type=MESH)
    for k in range(1, 8):
        pl.semaphore_signal(bar, inc=1, device_id=((me + k) % 8, y, z), device_id_type=MESH)
    local_copies = [
        pltpu.make_async_copy(cands.at[:, pl.ds(pl.multiple_of(core * 512, 512), 512)], shard, loc_sem.at[0]),
        pltpu.make_async_copy(cands.at[pl.ds(quarter * QUARTER, QUARTER)], held.at[pl.ds(0, QUARTER)], loc_sem.at[1]),
        pltpu.make_async_copy(points, pts.at[pl.ds(0, OWN)], loc_sem.at[2]),
    ]
    local_copies[0].start()
    sent[...] = jnp.zeros_like(sent)
    got[0] = jnp.zeros((8, BLK), jnp.float32)
    got[16] = jnp.zeros((8, BLK), jnp.float32)
    acc[...] = jnp.zeros_like(acc)
    sim1[...] = jnp.zeros_like(sim1)
    lists[0] = listed_own[...]

    local_copies[0].wait()
    for copy in local_copies[1:]:
        copy.start()
    row = lax.broadcasted_iota(jnp.int32, (16, ROWS), 0)
    lane = lax.broadcasted_iota(jnp.int32, (16, ROWS), 1)
    pick = jnp.zeros((16, ROWS), jnp.float32)
    for s in range(STEPS):
        wanted = lists[0, :, PROBES + s : PROBES + s + 1] - (y * 4 + z) * ROWS
        pick = jnp.where((row % 4 == s) & (lane == jnp.concatenate([wanted, wanted], axis=0)), 1.0, pick)
    mine = jnp.zeros((16, BLK), jnp.float32)
    for j in range(4):
        pick_j = jnp.where(row // 4 == j, pick, 0.0).astype(jnp.bfloat16)
        mine = mine + jnp.dot(pick_j, shard[:, j * BLK : (j + 1) * BLK], preferred_element_type=jnp.float32)
    fac[0] = mine.astype(jnp.bfloat16)

    pl.semaphore_wait(bar, 22)
    for dy, dz in others:
        fac_copy(dy, dz).start()
    list_copy(1, core).start()
    list_copy(0, core).start()
    go(key for key in FIRST if key[3] == 0)
    go(key for key in FIRST if key[3] == 1)
    go(ring(0, (3, 1), (0,)))
    go(ring(0, (3, 1), (1,)))
    for i in range(2):
        beside_copy(i).start()
    own_copy(0).start()
    own_copy(1).start()

    lane = lax.broadcasted_iota(jnp.int32, (8, GROUP), 1)
    for g in range(4):
        base = jnp.zeros((8, GROUP), jnp.int32)
        for i, (part, du, dv, h) in enumerate(ORDER[g * 16 : g * 16 + 16]):
            at_y, at_z = (y + (du, dv)[part]) % 4, (z + (dv, du)[part]) % 4
            begin = (at_y * 4 + at_z) * ROWS + quarter * QUARTER + part * PART + (h - i) * HALF
            base = jnp.where(lane >= i * HALF, begin, base)
        ids[g] = lax.shift_right_logical(base + lane, 7)

    def build_mask(unit, listed):
        for g in range(4):
            hit = ids[g] == listed[:, 0:1]
            for k in range(1, PROBES):
                hit = hit | (ids[g] == listed[:, k : k + 1])
            hit = jnp.where(hit, 1.0, 0.0)
            mask[unit, g, 0:4, :] = hit[0:4]
            mask[unit + 1, g, 0:4, :] = hit[4:8]

    build_mask(0, lists[0])
    list_copy(0, core).wait_recv()
    build_mask(2, lists[1])

    slots = fac.at[pl.ds(1, 15)]
    remote(slots, slots, fac_s, fac_r, sibling).wait_recv()
    whole = fac[0].astype(jnp.float32)
    for k in range(1, 16):
        whole = whole + fac[k].astype(jnp.float32)
    columns[core] = whole.astype(jnp.bfloat16)
    column_copy(core).start()
    list_copy(1, core).wait_recv()
    list_copy(2, core).start()
    column_copy(1 - core).wait_recv()
    pieces = [columns[side].astype(jnp.float32) for side in (0, 1)]
    wide = jnp.concatenate([piece if j == 0 else pltpu.roll(piece, 16 - 4 * j, 0) for piece in pieces for j in range(4)], axis=1).astype(jnp.bfloat16)
    for s in range(3):
        repeated[s * BLK : (s + 1) * BLK, :] = jnp.broadcast_to(wide[s : s + 1, :], (BLK, FEATURE))

    def thresholds(row, unit, sides):
        count = len(sides) * CHUNK
        fsim[0:count] = lax.dot_general(pts[pl.ds(row, count), :], repeated[...], NT, preferred_element_type=jnp.float32)
        for i, side in enumerate(sides):
            for q in range(2):
                sums = [jnp.zeros((8, BLK), jnp.float32) for _ in range(3)]
                for r in range(16):
                    at = i * CHUNK + q * BLK + r * 8
                    covered = jnp.zeros((8, BLK), jnp.float32)
                    for s in range(3):
                        covered = jnp.maximum(covered, fsim[at : at + 8, s * BLK : (s + 1) * BLK])
                        before[unit, s, side, q * BLK + r * 8 : q * BLK + r * 8 + 8, :] = covered
                        sums[s] = sums[s] + covered
                for s in range(3):
                    before[unit, s, side, CHUNK + q * 8 : CHUNK + q * 8 + 8, :] = sums[s]

    def beside_landed(i):
        beside_copy(i).wait_recv()
        pass_copy(i, core).start()
        thresholds(pl.multiple_of((4 + i) * UNIT + core * CHUNK, CHUNK), 4 + i, (core,))
        before_copy(i, core).start()

    def passed_landed(i):
        pass_copy(i, 1 - core).wait_recv()
        before_copy(i, 1 - core).wait_recv()

    for copy in local_copies[1:]:
        copy.wait()
    for unit in (0, 1):
        thresholds(unit * UNIT, unit, (0, 1))
        own_before_copy(unit).start()
    landed(0)
    go(OPPOSITE)
    for du in (1, 3):
        for h in (0, 1):
            go(ring(du, (3, 1), (h,)))
    all_own = pts.at[pl.ds(2 * UNIT, OWN)]
    remote(all_own, all_own, pt_s, pt_r, sibling).wait_recv()

    list_copy(2, 1 - core).wait_recv()
    left, right = lists[2], lists[3]
    build_mask(4, jnp.concatenate([left[0:2], right[0:2], left[2:4], right[2:4]], axis=0))
    build_mask(6, jnp.concatenate([left[4:6], right[4:6], left[6:8], right[6:8]], axis=0))

    facility_sim = lax.dot_general(wide, pts[0:OWN, :], NT, preferred_element_type=jnp.float32)
    covered = jnp.zeros((1, OWN), jnp.float32)
    for s in range(STEPS):
        covered = jnp.maximum(covered, facility_sim[s : s + 1, :])
    cover[...] = covered

    def send_gains(keys):
        totals = {}
        for part, du, dv in keys:
            pieces = []
            for h in (0, 1):
                g, i = divmod(POS[part, du, dv, h], 16)
                if g not in totals:
                    totals[g] = jnp.sum(acc[g], axis=1)
                pieces.append(totals[g][:, i * HALF : (i + 1) * HALF])
            slot = (part * 4 + du) * 4 + dv
            line = jnp.concatenate(pieces, axis=1)
            if (du, dv) == (0, 0):
                got[part * 16, 0:STEPS, 0:PART] = line
            else:
                sent[slot, 0:STEPS, 0:PART] = line
                gain_copy(part, du, dv).start()

    def e0():
        landed(1)

    def e1():
        beside_copy(2).start()
        beside_landed(0)
        theirs = before.at[pl.ds(2, 2)]
        remote(theirs, theirs, thr_s, thr_r, sibling).wait_recv()

    def e2():
        beside_landed(1)
        landed(2)
        go(ring(0, (2,), (0, 1)))
        go(ring(2, (3, 1), (0,)))
        go(ring(2, (3, 1), (1,)))
        passed_landed(0)
        passed_landed(1)

    def e3():
        beside_copy(3).start()
        landed(3)
        go(ring(1, (2,), (0, 1)))

    def e5():
        landed(4)
        go(ring(3, (2,), (0, 1)))
        beside_landed(2)

    def e6():
        passed_landed(2)

    def e7():
        landed(5)

    def e8():
        landed(6)
        go(ring(2, (2,), (0, 1)))

    def e9():
        beside_landed(3)

    def e10():
        passed_landed(3)

    def e12():
        landed(7)
        send_gains([(p, 3, dv) for p in (A, B) for dv in (3, 1)] + [(p, 0, 2) for p in (A, B)])

    def e13():
        send_gains([(p, du, 0) for p in (A, B) for du in (0, 1, 3, 2)] + [(p, du, dv) for p in (A, B) for du in (0, 1) for dv in (3, 1)])

    events = {0: e0, 1: e1, 2: e2, 3: e3, 5: e5, 6: e6, 7: e7, 8: e8, 9: e9, 10: e10, 12: e12, 13: e13}

    def prepare(i, low, high):
        if high - low == 1:
            if low in events:
                events[low]()
            return
        middle = (low + high) // 2
        pl.when(i < middle)(functools.partial(prepare, i, low, middle))
        pl.when(i >= middle)(functools.partial(prepare, i, middle, high))

    def product(t, sim):
        group, unit = tile_of(t)
        sim[...] = lax.dot_general(
            pts[pl.ds(pl.multiple_of(unit * UNIT, UNIT), UNIT), :], held[pl.ds(pl.multiple_of(group * GROUP, GROUP), GROUP), :],
            NT, preferred_element_type=jnp.float32)

    def hinge(t, sim):
        group, unit = tile_of(t)
        unit = jnp.where(t < 0, 0, unit)
        slot = jnp.where(t < 0, 4, group)
        for q in range(4):
            sums = [[None] * 6 for _ in range(STEPS)]
            for r in range(16):
                rows = slice(q * BLK + r * 8, q * BLK + r * 8 + 8)
                floors = [before[unit, s, q // 2, q % 2 * BLK + r * 8 : q % 2 * BLK + r * 8 + 8, :] for s in range(3)]
                for c in range(6):
                    value = sim[rows, c * BLK : (c + 1) * BLK]
                    tops = [jnp.maximum(value, 0.0)] + [jnp.maximum(value, floor) for floor in floors]
                    for s in range(STEPS):
                        sums[s][c] = tops[s] if r == 0 else sums[s][c] + tops[s]
            for c in range(6):
                cols = slice(c * BLK, (c + 1) * BLK)
                listed = mask[unit, group, q : q + 1, cols]
                for s in range(STEPS):
                    part = sums[s][c] if s == 0 else sums[s][c] - before[unit, s - 1, q // 2, CHUNK + q % 2 * 8 : CHUNK + q % 2 * 8 + 8, :]
                    acc[slot, s, :, cols] += part * listed

    def pair(i, _):
        t = i * 2
        prepare(i, 0, BLOCKS)
        product(t, sim0)
        hinge(t - 1, sim1)
        product(t + 1, sim1)
        hinge(t, sim0)
        return 0

    lax.fori_loop(0, BLOCKS, pair, 0)
    hinge(jnp.int32(2 * BLOCKS - 1), sim1)
    send_gains([(p, 2, dv) for p in (A, B) for dv in (3, 1)] + [(p, du, 2) for p in (A, B) for du in (1, 3, 2)])

    arrived = got.at[pl.ds(0, 30)]
    remote(arrived, arrived, red_s, red_r, sibling).wait_recv()
    for part in (A, B):
        total = got[part * 16]
        for k in range(1, 16):
            total = total + got[part * 16 + k]
        both[me, part] = total
    for k in range(1, 8):
        last_copy(k, me).start()
    seven = both.at[pl.ds(0, 7)]
    remote(seven, seven, last_s, last_r, sibling).wait_recv()
    for q in range(4):
        for part in (A, B):
            gains[q, part] = (both[q, part] + both[q + 4, part]) / (BLK * PROBES)

    for ref, send, recv in (
        (held.at[pl.ds(0, 60 * HALF)], cand_s, cand_r),
        (pts.at[pl.ds(0, 3 * OWN)], pt_s, pt_r),
        (slots, fac_s, fac_r),
        (columns.at[0], col_s, col_r),
        (lists.at[pl.ds(0, 3)], aux_s, aux_r),
        (before.at[pl.ds(0, 4)], thr_s, thr_r),
        (arrived, red_s, red_r),
        (seven, last_s, last_r),
    ):
        remote(ref, ref, send, recv, sibling).wait_send()


def local(points, candidates, probes, chosen):
    hbm, vmem = pl.BlockSpec(memory_space=pltpu.HBM), pl.BlockSpec(memory_space=pltpu.VMEM)
    f32, bf16, i32 = jnp.float32, jnp.bfloat16, jnp.int32
    dma = pltpu.SemaphoreType.DMA
    listed = jnp.pad(probes, ((0, 0), (0, BLK - PROBES))) + jnp.pad(chosen, (PROBES, BLK - PROBES - STEPS))[None, :]
    gains, cover = pl.pallas_call(
        kernel,
        out_shape=(jax.ShapeDtypeStruct((4, 2, 8, BLK), f32), jax.ShapeDtypeStruct((1, OWN), f32)),
        in_specs=[hbm, hbm, vmem],
        out_specs=(vmem, vmem),
        scratch_shapes=[
            pltpu.VMEM((4 * GROUP, FEATURE), bf16),
            pltpu.VMEM((8 * UNIT, FEATURE), bf16),
            pltpu.VMEM((ROWS, FEATURE // 2), bf16),
            pltpu.VMEM((5, STEPS, 8, GROUP), f32),
            pltpu.VMEM((8, 4, 8, GROUP), f32),
            pltpu.VMEM((8, 3, 2, CHUNK + 16, BLK), f32),
            pltpu.VMEM((UNIT, 3 * BLK), f32),
            pltpu.VMEM((UNIT, GROUP), f32),
            pltpu.VMEM((UNIT, GROUP), f32),
            pltpu.VMEM((4, 8, BLK), i32),
            pltpu.VMEM((4, 8, GROUP), i32),
            pltpu.VMEM((16, 16, BLK), bf16),
            pltpu.VMEM((2, 16, BLK), bf16),
            pltpu.VMEM((3 * BLK, FEATURE), bf16),
            pltpu.VMEM((32, 8, BLK), f32),
            pltpu.VMEM((32, 8, BLK), f32),
            pltpu.VMEM((8, 2, 8, BLK), f32),
            dma((3,)),
            dma((1,)), dma((8,)),
            dma((1,)), dma((1,)),
            dma((1,)), dma((1,)),
            dma((1,)), dma((9,)),
            dma((1,)), dma((3,)),
            dma((1,)), dma((5,)),
            dma((1,)), dma((1,)),
            dma((1,)), dma((1,)),
        ],
        compiler_params=pltpu.CompilerParams(collective_id=0, has_side_effects=True, vmem_limit_bytes=53 << 20),
        name="gather_gain",
    )(points, candidates, listed)
    gains = gains[:, :, :STEPS, :PART].transpose(2, 0, 1, 3).reshape(STEPS, ROWS)
    return (gains, cover.reshape(OWN))


def solution(mesh):
    return jax.shard_map(
        local,
        mesh=mesh,
        in_specs=(P(("pts", "ca", "cb"), None), P(("ca", "cb"), None), P(("pts", "ca", "cb"), None), P()),
        out_specs=(P(None, ("ca", "cb")), P(("pts", "ca", "cb"))),
        check_vma=False,
    )
```

```python
import functools

import jax
import jax.numpy as jnp
from jax import lax
from jax.experimental import pallas as pl
from jax.experimental.pallas import tpu as pltpu
from jax.sharding import PartitionSpec as P

BLK = 128
PROBES = 24
STEPS = 4
FEATURE = 1024
ROWS = 768
OWN = 1024
QUARTER = 192
PART = 96
HALF = 48
GROUP = 768
UNIT = 512
CHUNK = 256
BLOCKS = 16
NT = (((1,), (1,)), ((), ()))
MESH = pl.DeviceIdType.MESH
A, B = 0, 1


def halves(*keys):
    return [(part, du, dv, h) for part, du, dv in keys for h in (0, 1)]


def ring(du, dvs, hs):
    return [(part, du, dv, h) for part in (A, B) for dv in dvs for h in hs]


FIRST = halves((A, 1, 0), (A, 3, 0), (B, 1, 0), (B, 3, 0))
OPPOSITE = halves((A, 2, 0), (B, 2, 0))
ORDER = (
    halves((A, 0, 0), (B, 0, 0)) + FIRST + ring(0, (3, 1), (0,))
    + ring(0, (3, 1), (1,)) + OPPOSITE + ring(1, (3, 1), (0, 1))
    + ring(3, (3, 1), (0, 1)) + ring(0, (2,), (0, 1)) + ring(2, (3, 1), (0,))
    + ring(2, (3, 1), (1,)) + ring(1, (2,), (0, 1)) + ring(3, (2,), (0, 1)) + ring(2, (2,), (0, 1))
)
POS = {key: i for i, key in enumerate(ORDER)}
WAVES = (
    FIRST, ring(0, (3, 1), (0,)), ring(0, (3, 1), (1,)) + OPPOSITE, ring(1, (3, 1), (0, 1)),
    ring(3, (3, 1), (0, 1)), ring(0, (2,), (0, 1)) + ring(2, (3, 1), (0,)), ring(2, (3, 1), (1,)),
    ring(1, (2,), (0, 1)) + ring(3, (2,), (0, 1)) + ring(2, (2,), (0, 1)),
)
WAVE = {key: i for i, wave in enumerate(WAVES) for key in wave}


def tile_of(t):
    pick = jnp.where
    group = pick(t < 6, 0, pick(t < 12, 1, pick(t < 14, t - 12, pick(t < 22, 2, pick(t < 24, t - 22, 3)))))
    unit = pick(t < 6, t, pick(t < 12, t - 6, pick(t < 14, 6, pick(t < 22, t - 14, pick(t < 24, 7, t - 24)))))
    return group, unit


def kernel(
    points, cands, listed_own, gains, cover,
    held, pts, shard, acc, mask, before, fsim, sim0, sim1, lists, ids, fac, columns, repeated, sent, got, both,
    loc_sem, cand_s, cand_r, fac_s, fac_r, col_s, col_r, pt_s, pt_r, aux_s, aux_r, thr_s, thr_r, red_s, red_r, last_s, last_r,
):
    me = lax.axis_index("pts")
    y = lax.axis_index("ca")
    z = lax.axis_index("cb")
    x, core = me // 2, me % 2
    quarter = 2 * (x % 2) + core
    way = 1 - 2 * core

    def plane(dy, dz):
        return (me, (y + dy + 4) % 4, (z + dz + 4) % 4)

    sibling = (2 * x + 1 - core, y, z)
    beside = (2 * ((x + way + 4) % 4) + core, y, z)

    def along(part, du, dv):
        return plane(du, dv) if part == A else plane(dv, du)

    def remote(src, dst, send, recv, device, k=0):
        return pltpu.make_async_remote_copy(src_ref=src, dst_ref=dst, send_sem=send.at[0], recv_sem=recv.at[k], device_id=device, device_id_type=MESH)

    def cand_copy(part, du, dv, half):
        row = POS[part, du, dv, half] * HALF
        if dv == 0:
            hop_u, hop_v = {1: -1, 3: 1, 2: (1 if half == 0 else -1)}[du], 0
            source = (part, 0, 0) if du != 2 else (part, 3 if half == 0 else 1, 0)
        else:
            hop_u, hop_v = 0, {1: -1, 3: 1, 2: (1 if half == 0 else -1)}[dv]
            source = (part, du, 0) if dv != 2 else (part, du, 3 if half == 0 else 1)
        if source[1:] == (0, 0):
            src = cands.at[pl.ds(quarter * QUARTER + part * PART + half * HALF, HALF)]
        else:
            src = held.at[pl.ds(POS[source + (half,)] * HALF, HALF)]
        return remote(src, held.at[pl.ds(row, HALF)], cand_s, cand_r, along(part, hop_u, hop_v), WAVE[part, du, dv, half])

    def go(keys):
        for key in keys:
            cand_copy(*key).start()

    def landed(wave):
        at = [i for i, key in enumerate(ORDER) if WAVE.get(key) == wave]
        rows = held.at[pl.ds(at[0] * HALF, len(at) * HALF)]
        remote(rows, rows, cand_s, cand_r, sibling, wave).wait_recv()

    def fac_copy(dy, dz):
        k = ((4 - dy) % 4) * 4 + (4 - dz) % 4
        return remote(fac.at[0], fac.at[k], fac_s, fac_r, plane(dy, dz))

    def column_copy(side):
        return remote(columns.at[side], columns.at[side], col_s, col_r, sibling)

    def own_copy(i):
        return remote(points.at[pl.ds(i * UNIT, UNIT)], pts.at[pl.ds((2 + i) * UNIT, UNIT)], pt_s, pt_r, sibling)

    def chunk_at(i, side):
        return pts.at[pl.ds((4 + i) * UNIT + side * CHUNK, CHUNK)]

    def beside_copy(i):
        return remote(points.at[pl.ds(i * CHUNK, CHUNK)], chunk_at(i, core), pt_s, pt_r, beside, 1 + i)

    def pass_copy(i, side):
        return remote(chunk_at(i, side), chunk_at(i, side), pt_s, pt_r, sibling, 5 + i)

    def list_copy(kind, side):
        if kind == 0:
            return remote(lists.at[0], lists.at[1], aux_s, aux_r, sibling)
        if kind == 1:
            return remote(lists.at[0], lists.at[2 + side], aux_s, aux_r, beside, 1)
        return remote(lists.at[2 + side], lists.at[2 + side], aux_s, aux_r, sibling, 2)

    def own_before_copy(unit):
        return remote(before.at[unit], before.at[2 + unit], thr_s, thr_r, sibling)

    def before_copy(i, side):
        here = before.at[4 + i, :, side]
        return remote(here, here, thr_s, thr_r, sibling, 1 + i)

    def gain_copy(part, du, dv):
        k = part * 16 + ((4 - du) % 4) * 4 + (4 - dv) % 4
        return remote(sent.at[(part * 4 + du) * 4 + dv], got.at[k], red_s, red_r, along(part, du, dv))

    def last_copy(k, slot):
        return remote(both.at[slot], both.at[slot], last_s, last_r, ((me + k) % 8, y, z))

    bar = pltpu.get_barrier_semaphore()
    others = [(dy, dz) for dy in range(4) for dz in range(4) if (dy, dz) != (0, 0)]
    for dy, dz in others:
        pl.semaphore_signal(bar, inc=1, device_id=plane(dy, dz), device_id_type=MESH)
    for k in range(1, 8):
        pl.semaphore_signal(bar, inc=1, device_id=((me + k) % 8, y, z), device_id_type=MESH)
    local_copies = [
        pltpu.make_async_copy(cands.at[:, pl.ds(pl.multiple_of(core * 512, 512), 512)], shard, loc_sem.at[0]),
        pltpu.make_async_copy(cands.at[pl.ds(quarter * QUARTER, QUARTER)], held.at[pl.ds(0, QUARTER)], loc_sem.at[1]),
        pltpu.make_async_copy(points, pts.at[pl.ds(0, OWN)], loc_sem.at[2]),
    ]
    local_copies[0].start()
    sent[...] = jnp.zeros_like(sent)
    got[0] = jnp.zeros((8, BLK), jnp.float32)
    got[16] = jnp.zeros((8, BLK), jnp.float32)
    acc[...] = jnp.zeros_like(acc)
    sim1[...] = jnp.zeros_like(sim1)
    lists[0] = listed_own[...]

    local_copies[0].wait()
    for copy in local_copies[1:]:
        copy.start()
    row = lax.broadcasted_iota(jnp.int32, (16, ROWS), 0)
    lane = lax.broadcasted_iota(jnp.int32, (16, ROWS), 1)
    pick = jnp.zeros((16, ROWS), jnp.float32)
    for s in range(STEPS):
        wanted = lists[0, :, PROBES + s : PROBES + s + 1] - (y * 4 + z) * ROWS
        pick = jnp.where((row % 4 == s) & (lane == jnp.concatenate([wanted, wanted], axis=0)), 1.0, pick)
    mine = jnp.zeros((16, BLK), jnp.float32)
    for j in range(4):
        pick_j = jnp.where(row // 4 == j, pick, 0.0).astype(jnp.bfloat16)
        mine = mine + jnp.dot(pick_j, shard[:, j * BLK : (j + 1) * BLK], preferred_element_type=jnp.float32)
    fac[0] = mine.astype(jnp.bfloat16)

    pl.semaphore_wait(bar, 22)
    for dy, dz in others:
        fac_copy(dy, dz).start()
    list_copy(1, core).start()
    list_copy(0, core).start()
    go(key for key in FIRST if key[3] == 0)
    go(key for key in FIRST if key[3] == 1)
    go(ring(0, (3, 1), (0,)))
    go(ring(0, (3, 1), (1,)))
    for i in range(2):
        beside_copy(i).start()
    own_copy(0).start()
    own_copy(1).start()

    lane = lax.broadcasted_iota(jnp.int32, (8, GROUP), 1)
    for g in range(4):
        base = jnp.zeros((8, GROUP), jnp.int32)
        for i, (part, du, dv, h) in enumerate(ORDER[g * 16 : g * 16 + 16]):
            at_y, at_z = (y + (du, dv)[part]) % 4, (z + (dv, du)[part]) % 4
            begin = (at_y * 4 + at_z) * ROWS + quarter * QUARTER + part * PART + (h - i) * HALF
            base = jnp.where(lane >= i * HALF, begin, base)
        ids[g] = lax.shift_right_logical(base + lane, 7)

    def build_mask(unit, listed):
        for g in range(4):
            hit = ids[g] == listed[:, 0:1]
            for k in range(1, PROBES):
                hit = hit | (ids[g] == listed[:, k : k + 1])
            hit = jnp.where(hit, 1.0, 0.0)
            mask[unit, g, 0:4, :] = hit[0:4]
            mask[unit + 1, g, 0:4, :] = hit[4:8]

    build_mask(0, lists[0])
    list_copy(0, core).wait_recv()
    build_mask(2, lists[1])

    slots = fac.at[pl.ds(1, 15)]
    remote(slots, slots, fac_s, fac_r, sibling).wait_recv()
    whole = fac[0].astype(jnp.float32)
    for k in range(1, 16):
        whole = whole + fac[k].astype(jnp.float32)
    columns[core] = whole.astype(jnp.bfloat16)
    column_copy(core).start()
    list_copy(1, core).wait_recv()
    list_copy(2, core).start()
    column_copy(1 - core).wait_recv()
    pieces = [columns[side].astype(jnp.float32) for side in (0, 1)]
    wide = jnp.concatenate([piece if j == 0 else pltpu.roll(piece, 16 - 4 * j, 0) for piece in pieces for j in range(4)], axis=1).astype(jnp.bfloat16)
    for s in range(3):
        repeated[s * BLK : (s + 1) * BLK, :] = jnp.broadcast_to(wide[s : s + 1, :], (BLK, FEATURE))

    def thresholds(row, unit, sides):
        count = len(sides) * CHUNK
        fsim[0:count] = lax.dot_general(pts[pl.ds(row, count), :], repeated[...], NT, preferred_element_type=jnp.float32)
        for i, side in enumerate(sides):
            for q in range(2):
                sums = [jnp.zeros((8, BLK), jnp.float32) for _ in range(3)]
                for r in range(16):
                    at = i * CHUNK + q * BLK + r * 8
                    covered = jnp.zeros((8, BLK), jnp.float32)
                    for s in range(3):
                        covered = jnp.maximum(covered, fsim[at : at + 8, s * BLK : (s + 1) * BLK])
                        before[unit, s, side, q * BLK + r * 8 : q * BLK + r * 8 + 8, :] = covered
                        sums[s] = sums[s] + covered
                for s in range(3):
                    before[unit, s, side, CHUNK + q * 8 : CHUNK + q * 8 + 8, :] = sums[s]

    def beside_landed(i):
        beside_copy(i).wait_recv()
        pass_copy(i, core).start()
        thresholds(pl.multiple_of((4 + i) * UNIT + core * CHUNK, CHUNK), 4 + i, (core,))
        before_copy(i, core).start()

    def passed_landed(i):
        pass_copy(i, 1 - core).wait_recv()
        before_copy(i, 1 - core).wait_recv()

    for copy in local_copies[1:]:
        copy.wait()
    for unit in (0, 1):
        thresholds(unit * UNIT, unit, (0, 1))
        own_before_copy(unit).start()
    landed(0)
    go(OPPOSITE)
    for du in (1, 3):
        for h in (0, 1):
            go(ring(du, (3, 1), (h,)))
    all_own = pts.at[pl.ds(2 * UNIT, OWN)]
    remote(all_own, all_own, pt_s, pt_r, sibling).wait_recv()

    list_copy(2, 1 - core).wait_recv()
    left, right = lists[2], lists[3]
    build_mask(4, jnp.concatenate([left[0:2], right[0:2], left[2:4], right[2:4]], axis=0))
    build_mask(6, jnp.concatenate([left[4:6], right[4:6], left[6:8], right[6:8]], axis=0))

    facility_sim = lax.dot_general(wide, pts[0:OWN, :], NT, preferred_element_type=jnp.float32)
    covered = jnp.zeros((1, OWN), jnp.float32)
    for s in range(STEPS):
        covered = jnp.maximum(covered, facility_sim[s : s + 1, :])
    cover[...] = covered

    def send_gains(keys):
        totals = {}
        for part, du, dv in keys:
            pieces = []
            for h in (0, 1):
                g, i = divmod(POS[part, du, dv, h], 16)
                if g not in totals:
                    totals[g] = jnp.sum(acc[g], axis=1)
                pieces.append(totals[g][:, i * HALF : (i + 1) * HALF])
            slot = (part * 4 + du) * 4 + dv
            line = jnp.concatenate(pieces, axis=1)
            if (du, dv) == (0, 0):
                got[part * 16, 0:STEPS, 0:PART] = line
            else:
                sent[slot, 0:STEPS, 0:PART] = line
                gain_copy(part, du, dv).start()

    def e0():
        landed(1)

    def e1():
        beside_copy(2).start()
        beside_landed(0)
        theirs = before.at[pl.ds(2, 2)]
        remote(theirs, theirs, thr_s, thr_r, sibling).wait_recv()

    def e2():
        beside_landed(1)
        landed(2)
        go(ring(0, (2,), (0, 1)))
        go(ring(2, (3, 1), (0,)))
        go(ring(2, (3, 1), (1,)))
        passed_landed(0)
        pass_copy(1, 1 - core).wait_recv()

    def e3():
        beside_copy(3).start()
        before_copy(1, 1 - core).wait_recv()
        landed(3)
        go(ring(1, (2,), (0, 1)))

    def e5():
        landed(4)
        go(ring(3, (2,), (0, 1)))
        beside_landed(2)

    def e6():
        passed_landed(2)

    def e7():
        landed(5)

    def e8():
        landed(6)
        go(ring(2, (2,), (0, 1)))

    def e9():
        beside_landed(3)

    def e10():
        pass_copy(3, 1 - core).wait_recv()

    def e11():
        before_copy(3, 1 - core).wait_recv()

    def e12():
        landed(7)
        send_gains([(p, 3, dv) for p in (A, B) for dv in (3, 1)] + [(p, 0, 2) for p in (A, B)])

    def e13():
        send_gains([(p, du, 0) for p in (A, B) for du in (0, 1, 3, 2)] + [(p, du, dv) for p in (A, B) for du in (0, 1) for dv in (3, 1)])

    events = {0: e0, 1: e1, 2: e2, 3: e3, 5: e5, 6: e6, 7: e7, 8: e8, 9: e9, 10: e10, 11: e11, 12: e12, 13: e13}

    def prepare(i, low, high):
        if high - low == 1:
            if low in events:
                events[low]()
            return
        middle = (low + high) // 2
        pl.when(i < middle)(functools.partial(prepare, i, low, middle))
        pl.when(i >= middle)(functools.partial(prepare, i, middle, high))

    def product(t, sim):
        group, unit = tile_of(t)
        sim[...] = lax.dot_general(
            pts[pl.ds(pl.multiple_of(unit * UNIT, UNIT), UNIT), :], held[pl.ds(pl.multiple_of(group * GROUP, GROUP), GROUP), :],
            NT, preferred_element_type=jnp.float32)

    def hinge(t, sim):
        group, unit = tile_of(t)
        unit = jnp.where(t < 0, 0, unit)
        slot = jnp.where(t < 0, 4, group)
        for q in range(4):
            sums = [[None] * 6 for _ in range(STEPS)]
            for r in range(16):
                rows = slice(q * BLK + r * 8, q * BLK + r * 8 + 8)
                floors = [before[unit, s, q // 2, q % 2 * BLK + r * 8 : q % 2 * BLK + r * 8 + 8, :] for s in range(3)]
                for c in range(6):
                    value = sim[rows, c * BLK : (c + 1) * BLK]
                    tops = [jnp.maximum(value, 0.0)] + [jnp.maximum(value, floor) for floor in floors]
                    for s in range(STEPS):
                        sums[s][c] = tops[s] if r == 0 else sums[s][c] + tops[s]
            for c in range(6):
                cols = slice(c * BLK, (c + 1) * BLK)
                listed = mask[unit, group, q : q + 1, cols]
                for s in range(STEPS):
                    part = sums[s][c] if s == 0 else sums[s][c] - before[unit, s - 1, q // 2, CHUNK + q % 2 * 8 : CHUNK + q % 2 * 8 + 8, :]
                    acc[slot, s, :, cols] += part * listed

    def pair(i, _):
        t = i * 2
        prepare(i, 0, BLOCKS)
        product(t, sim0)
        hinge(t - 1, sim1)
        product(t + 1, sim1)
        hinge(t, sim0)
        return 0

    lax.fori_loop(0, BLOCKS, pair, 0)
    hinge(jnp.int32(2 * BLOCKS - 1), sim1)
    send_gains([(p, 2, dv) for p in (A, B) for dv in (3, 1)] + [(p, du, 2) for p in (A, B) for du in (1, 3, 2)])

    arrived = got.at[pl.ds(0, 30)]
    remote(arrived, arrived, red_s, red_r, sibling).wait_recv()
    for part in (A, B):
        total = got[part * 16]
        for k in range(1, 16):
            total = total + got[part * 16 + k]
        both[me, part] = total
    for k in range(1, 8):
        last_copy(k, me).start()
    seven = both.at[pl.ds(0, 7)]
    remote(seven, seven, last_s, last_r, sibling).wait_recv()
    for q in range(4):
        for part in (A, B):
            gains[q, part] = (both[q, part] + both[q + 4, part]) / (BLK * PROBES)

    for ref, send, recv in (
        (held.at[pl.ds(0, 60 * HALF)], cand_s, cand_r),
        (pts.at[pl.ds(0, 3 * OWN)], pt_s, pt_r),
        (slots, fac_s, fac_r),
        (columns.at[0], col_s, col_r),
        (lists.at[pl.ds(0, 3)], aux_s, aux_r),
        (before.at[pl.ds(0, 4)], thr_s, thr_r),
        (arrived, red_s, red_r),
        (seven, last_s, last_r),
    ):
        remote(ref, ref, send, recv, sibling).wait_send()


def local(points, candidates, probes, chosen):
    hbm, vmem = pl.BlockSpec(memory_space=pltpu.HBM), pl.BlockSpec(memory_space=pltpu.VMEM)
    f32, bf16, i32 = jnp.float32, jnp.bfloat16, jnp.int32
    dma = pltpu.SemaphoreType.DMA
    listed = jnp.pad(probes, ((0, 0), (0, BLK - PROBES))) + jnp.pad(chosen, (PROBES, BLK - PROBES - STEPS))[None, :]
    gains, cover = pl.pallas_call(
        kernel,
        out_shape=(jax.ShapeDtypeStruct((4, 2, 8, BLK), f32), jax.ShapeDtypeStruct((1, OWN), f32)),
        in_specs=[hbm, hbm, vmem],
        out_specs=(vmem, vmem),
        scratch_shapes=[
            pltpu.VMEM((4 * GROUP, FEATURE), bf16),
            pltpu.VMEM((8 * UNIT, FEATURE), bf16),
            pltpu.VMEM((ROWS, FEATURE // 2), bf16),
            pltpu.VMEM((5, STEPS, 8, GROUP), f32),
            pltpu.VMEM((8, 4, 8, GROUP), f32),
            pltpu.VMEM((8, 3, 2, CHUNK + 16, BLK), f32),
            pltpu.VMEM((UNIT, 3 * BLK), f32),
            pltpu.VMEM((UNIT, GROUP), f32),
            pltpu.VMEM((UNIT, GROUP), f32),
            pltpu.VMEM((4, 8, BLK), i32),
            pltpu.VMEM((4, 8, GROUP), i32),
            pltpu.VMEM((16, 16, BLK), bf16),
            pltpu.VMEM((2, 16, BLK), bf16),
            pltpu.VMEM((3 * BLK, FEATURE), bf16),
            pltpu.VMEM((32, 8, BLK), f32),
            pltpu.VMEM((32, 8, BLK), f32),
            pltpu.VMEM((8, 2, 8, BLK), f32),
            dma((3,)),
            dma((1,)), dma((8,)),
            dma((1,)), dma((1,)),
            dma((1,)), dma((1,)),
            dma((1,)), dma((9,)),
            dma((1,)), dma((3,)),
            dma((1,)), dma((5,)),
            dma((1,)), dma((1,)),
            dma((1,)), dma((1,)),
        ],
        compiler_params=pltpu.CompilerParams(collective_id=0, has_side_effects=True, vmem_limit_bytes=53 << 20),
        name="gather_gain",
    )(points, candidates, listed)
    gains = gains[:, :, :STEPS, :PART].transpose(2, 0, 1, 3).reshape(STEPS, ROWS)
    return (gains, cover.reshape(OWN))


def solution(mesh):
    return jax.shard_map(
        local,
        mesh=mesh,
        in_specs=(P(("pts", "ca", "cb"), None), P(("ca", "cb"), None), P(("pts", "ca", "cb"), None), P()),
        out_specs=(P(None, ("ca", "cb")), P(("pts", "ca", "cb"))),
        check_vma=False,
    )
```

```python
import functools

import jax
import jax.numpy as jnp
from jax import lax
from jax.experimental import pallas as pl
from jax.experimental.pallas import tpu as pltpu
from jax.sharding import PartitionSpec as P

BLK = 128
PROBES = 24
STEPS = 4
FEATURE = 1024
ROWS = 768
OWN = 1024
QUARTER = 192
PART = 96
HALF = 48
GROUP = 768
UNIT = 512
CHUNK = 256
BLOCKS = 16
NT = (((1,), (1,)), ((), ()))
MESH = pl.DeviceIdType.MESH
A, B = 0, 1


def halves(*keys):
    return [(part, du, dv, h) for part, du, dv in keys for h in (0, 1)]


def ring(du, dvs, hs):
    return [(part, du, dv, h) for part in (A, B) for dv in dvs for h in hs]


FIRST = halves((A, 1, 0), (A, 3, 0), (B, 1, 0), (B, 3, 0))
OPPOSITE = halves((A, 2, 0), (B, 2, 0))
ORDER = (
    halves((A, 0, 0), (B, 0, 0)) + FIRST + ring(0, (3, 1), (0,))
    + ring(0, (3, 1), (1,)) + OPPOSITE + ring(1, (3, 1), (0, 1))
    + ring(3, (3, 1), (0, 1)) + ring(0, (2,), (0, 1)) + ring(2, (3, 1), (0,))
    + ring(2, (3, 1), (1,)) + ring(1, (2,), (0, 1)) + ring(3, (2,), (0, 1)) + ring(2, (2,), (0, 1))
)
POS = {key: i for i, key in enumerate(ORDER)}
WAVES = (
    FIRST, ring(0, (3, 1), (0,)), ring(0, (3, 1), (1,)) + OPPOSITE, ring(1, (3, 1), (0, 1)),
    ring(3, (3, 1), (0, 1)), ring(0, (2,), (0, 1)) + ring(2, (3, 1), (0,)), ring(2, (3, 1), (1,)),
    ring(1, (2,), (0, 1)) + ring(3, (2,), (0, 1)) + ring(2, (2,), (0, 1)),
)
WAVE = {key: i for i, wave in enumerate(WAVES) for key in wave}


def tile_of(t):
    pick = jnp.where
    group = pick(t < 6, 0, pick(t < 12, 1, pick(t < 14, t - 12, pick(t < 22, 2, pick(t < 24, t - 22, 3)))))
    unit = pick(t < 6, t, pick(t < 12, t - 6, pick(t < 14, 6, pick(t < 22, t - 14, pick(t < 24, 7, t - 24)))))
    return group, unit


def kernel(
    points, cands, listed_own, gains, cover,
    held, pts, shard, acc, mask, before, fsim, sim0, sim1, lists, ids, fac, columns, repeated, sent, got, both,
    loc_sem, cand_s, cand_r, fac_s, fac_r, col_s, col_r, pt_s, pt_r, aux_s, aux_r, thr_s, thr_r, red_s, red_r, last_s, last_r,
):
    me = lax.axis_index("pts")
    y = lax.axis_index("ca")
    z = lax.axis_index("cb")
    x, core = me // 2, me % 2
    quarter = 2 * (x % 2) + core
    way = 1 - 2 * core

    def plane(dy, dz):
        return (me, (y + dy + 4) % 4, (z + dz + 4) % 4)

    sibling = (2 * x + 1 - core, y, z)
    beside = (2 * ((x + way + 4) % 4) + core, y, z)

    def along(part, du, dv):
        return plane(du, dv) if part == A else plane(dv, du)

    def remote(src, dst, send, recv, device, k=0):
        return pltpu.make_async_remote_copy(src_ref=src, dst_ref=dst, send_sem=send.at[0], recv_sem=recv.at[k], device_id=device, device_id_type=MESH)

    def cand_copy(part, du, dv, half):
        row = POS[part, du, dv, half] * HALF
        if dv == 0:
            hop_u, hop_v = {1: -1, 3: 1, 2: (1 if half == 0 else -1)}[du], 0
            source = (part, 0, 0) if du != 2 else (part, 3 if half == 0 else 1, 0)
        else:
            hop_u, hop_v = 0, {1: -1, 3: 1, 2: (1 if half == 0 else -1)}[dv]
            source = (part, du, 0) if dv != 2 else (part, du, 3 if half == 0 else 1)
        if source[1:] == (0, 0):
            src = cands.at[pl.ds(quarter * QUARTER + part * PART + half * HALF, HALF)]
        else:
            src = held.at[pl.ds(POS[source + (half,)] * HALF, HALF)]
        return remote(src, held.at[pl.ds(row, HALF)], cand_s, cand_r, along(part, hop_u, hop_v), WAVE[part, du, dv, half])

    def go(keys):
        for key in keys:
            cand_copy(*key).start()

    def landed(wave):
        at = [i for i, key in enumerate(ORDER) if WAVE.get(key) == wave]
        rows = held.at[pl.ds(at[0] * HALF, len(at) * HALF)]
        remote(rows, rows, cand_s, cand_r, sibling, wave).wait_recv()

    def fac_copy(dy, dz):
        k = ((4 - dy) % 4) * 4 + (4 - dz) % 4
        return remote(fac.at[0], fac.at[k], fac_s, fac_r, plane(dy, dz))

    def column_copy(side):
        return remote(columns.at[side], columns.at[side], col_s, col_r, sibling)

    def own_copy(i):
        return remote(points.at[pl.ds(i * UNIT, UNIT)], pts.at[pl.ds((2 + i) * UNIT, UNIT)], pt_s, pt_r, sibling)

    def chunk_at(i, side):
        return pts.at[pl.ds((4 + i) * UNIT + side * CHUNK, CHUNK)]

    def beside_copy(i):
        return remote(points.at[pl.ds(i * CHUNK, CHUNK)], chunk_at(i, core), pt_s, pt_r, beside, 1 + i)

    def pass_copy(i, side):
        return remote(chunk_at(i, side), chunk_at(i, side), pt_s, pt_r, sibling, 5 + i)

    def list_copy(kind, side):
        if kind == 0:
            return remote(lists.at[0], lists.at[1], aux_s, aux_r, sibling)
        if kind == 1:
            return remote(lists.at[0], lists.at[2 + side], aux_s, aux_r, beside, 1)
        return remote(lists.at[2 + side], lists.at[2 + side], aux_s, aux_r, sibling, 2)

    def own_before_copy(unit):
        return remote(before.at[unit], before.at[2 + unit], thr_s, thr_r, sibling)

    def before_copy(i, side):
        here = before.at[4 + i, :, side]
        return remote(here, here, thr_s, thr_r, sibling, 1 + i)

    def gain_copy(part, du, dv):
        k = part * 16 + ((4 - du) % 4) * 4 + (4 - dv) % 4
        return remote(sent.at[(part * 4 + du) * 4 + dv], got.at[k], red_s, red_r, along(part, du, dv))

    def last_copy(k, slot):
        return remote(both.at[slot], both.at[slot], last_s, last_r, ((me + k) % 8, y, z))

    bar = pltpu.get_barrier_semaphore()
    others = [(dy, dz) for dy in range(4) for dz in range(4) if (dy, dz) != (0, 0)]
    for dy, dz in others:
        pl.semaphore_signal(bar, inc=1, device_id=plane(dy, dz), device_id_type=MESH)
    for k in range(1, 8):
        pl.semaphore_signal(bar, inc=1, device_id=((me + k) % 8, y, z), device_id_type=MESH)
    local_copies = [
        pltpu.make_async_copy(cands.at[:, pl.ds(pl.multiple_of(core * 512, 512), 512)], shard, loc_sem.at[0]),
        pltpu.make_async_copy(cands.at[pl.ds(quarter * QUARTER, QUARTER)], held.at[pl.ds(0, QUARTER)], loc_sem.at[1]),
        pltpu.make_async_copy(points, pts.at[pl.ds(0, OWN)], loc_sem.at[2]),
    ]
    local_copies[0].start()
    sent[...] = jnp.zeros_like(sent)
    got[0] = jnp.zeros((8, BLK), jnp.float32)
    got[16] = jnp.zeros((8, BLK), jnp.float32)
    acc[...] = jnp.zeros_like(acc)
    sim1[...] = jnp.zeros_like(sim1)
    lists[0] = listed_own[...]

    local_copies[0].wait()
    for copy in local_copies[1:]:
        copy.start()
    row = lax.broadcasted_iota(jnp.int32, (16, ROWS), 0)
    lane = lax.broadcasted_iota(jnp.int32, (16, ROWS), 1)
    pick = jnp.zeros((16, ROWS), jnp.float32)
    for s in range(STEPS):
        wanted = lists[0, :, PROBES + s : PROBES + s + 1] - (y * 4 + z) * ROWS
        pick = jnp.where((row % 4 == s) & (lane == jnp.concatenate([wanted, wanted], axis=0)), 1.0, pick)
    mine = jnp.zeros((16, BLK), jnp.float32)
    for j in range(4):
        pick_j = jnp.where(row // 4 == j, pick, 0.0).astype(jnp.bfloat16)
        mine = mine + jnp.dot(pick_j, shard[:, j * BLK : (j + 1) * BLK], preferred_element_type=jnp.float32)
    fac[0] = mine.astype(jnp.bfloat16)

    pl.semaphore_wait(bar, 22)
    list_copy(1, core).start()
    list_copy(0, core).start()
    for i in range(2):
        beside_copy(i).start()
    for dy, dz in others:
        fac_copy(dy, dz).start()
    go(key for key in FIRST if key[3] == 0)
    go(key for key in FIRST if key[3] == 1)
    go(ring(0, (3, 1), (0,)))
    go(ring(0, (3, 1), (1,)))
    own_copy(0).start()
    own_copy(1).start()

    lane = lax.broadcasted_iota(jnp.int32, (8, GROUP), 1)
    for g in range(4):
        base = jnp.zeros((8, GROUP), jnp.int32)
        for i, (part, du, dv, h) in enumerate(ORDER[g * 16 : g * 16 + 16]):
            at_y, at_z = (y + (du, dv)[part]) % 4, (z + (dv, du)[part]) % 4
            begin = (at_y * 4 + at_z) * ROWS + quarter * QUARTER + part * PART + (h - i) * HALF
            base = jnp.where(lane >= i * HALF, begin, base)
        ids[g] = lax.shift_right_logical(base + lane, 7)

    def build_mask(unit, listed):
        for g in range(4):
            hit = ids[g] == listed[:, 0:1]
            for k in range(1, PROBES):
                hit = hit | (ids[g] == listed[:, k : k + 1])
            hit = jnp.where(hit, 1.0, 0.0)
            mask[unit, g, 0:4, :] = hit[0:4]
            mask[unit + 1, g, 0:4, :] = hit[4:8]

    build_mask(0, lists[0])
    list_copy(0, core).wait_recv()
    build_mask(2, lists[1])

    slots = fac.at[pl.ds(1, 15)]
    remote(slots, slots, fac_s, fac_r, sibling).wait_recv()
    whole = fac[0].astype(jnp.float32)
    for k in range(1, 16):
        whole = whole + fac[k].astype(jnp.float32)
    columns[core] = whole.astype(jnp.bfloat16)
    column_copy(core).start()
    list_copy(1, core).wait_recv()
    list_copy(2, core).start()
    column_copy(1 - core).wait_recv()
    pieces = [columns[side].astype(jnp.float32) for side in (0, 1)]
    wide = jnp.concatenate([piece if j == 0 else pltpu.roll(piece, 16 - 4 * j, 0) for piece in pieces for j in range(4)], axis=1).astype(jnp.bfloat16)
    for s in range(3):
        repeated[s * BLK : (s + 1) * BLK, :] = jnp.broadcast_to(wide[s : s + 1, :], (BLK, FEATURE))

    def thresholds(row, unit, sides):
        count = len(sides) * CHUNK
        fsim[0:count] = lax.dot_general(pts[pl.ds(row, count), :], repeated[...], NT, preferred_element_type=jnp.float32)
        for i, side in enumerate(sides):
            for q in range(2):
                sums = [jnp.zeros((8, BLK), jnp.float32) for _ in range(3)]
                for r in range(16):
                    at = i * CHUNK + q * BLK + r * 8
                    covered = jnp.zeros((8, BLK), jnp.float32)
                    for s in range(3):
                        covered = jnp.maximum(covered, fsim[at : at + 8, s * BLK : (s + 1) * BLK])
                        before[unit, s, side, q * BLK + r * 8 : q * BLK + r * 8 + 8, :] = covered
                        sums[s] = sums[s] + covered
                for s in range(3):
                    before[unit, s, side, CHUNK + q * 8 : CHUNK + q * 8 + 8, :] = sums[s]

    def beside_landed(i):
        beside_copy(i).wait_recv()
        pass_copy(i, core).start()
        thresholds(pl.multiple_of((4 + i) * UNIT + core * CHUNK, CHUNK), 4 + i, (core,))
        before_copy(i, core).start()

    def passed_landed(i):
        pass_copy(i, 1 - core).wait_recv()
        before_copy(i, 1 - core).wait_recv()

    for copy in local_copies[1:]:
        copy.wait()
    for unit in (0, 1):
        thresholds(unit * UNIT, unit, (0, 1))
        own_before_copy(unit).start()
    landed(0)
    go(OPPOSITE)
    for du in (1, 3):
        for h in (0, 1):
            go(ring(du, (3, 1), (h,)))
    all_own = pts.at[pl.ds(2 * UNIT, OWN)]
    remote(all_own, all_own, pt_s, pt_r, sibling).wait_recv()

    list_copy(2, 1 - core).wait_recv()
    left, right = lists[2], lists[3]
    build_mask(4, jnp.concatenate([left[0:2], right[0:2], left[2:4], right[2:4]], axis=0))
    build_mask(6, jnp.concatenate([left[4:6], right[4:6], left[6:8], right[6:8]], axis=0))

    facility_sim = lax.dot_general(wide, pts[0:OWN, :], NT, preferred_element_type=jnp.float32)
    covered = jnp.zeros((1, OWN), jnp.float32)
    for s in range(STEPS):
        covered = jnp.maximum(covered, facility_sim[s : s + 1, :])
    cover[...] = covered

    def send_gains(keys):
        totals = {}
        for part, du, dv in keys:
            pieces = []
            for h in (0, 1):
                g, i = divmod(POS[part, du, dv, h], 16)
                if g not in totals:
                    totals[g] = jnp.sum(acc[g], axis=1)
                pieces.append(totals[g][:, i * HALF : (i + 1) * HALF])
            slot = (part * 4 + du) * 4 + dv
            line = jnp.concatenate(pieces, axis=1)
            if (du, dv) == (0, 0):
                got[part * 16, 0:STEPS, 0:PART] = line
            else:
                sent[slot, 0:STEPS, 0:PART] = line
                gain_copy(part, du, dv).start()

    def e0():
        landed(1)

    def e1():
        beside_copy(2).start()
        beside_landed(0)
        theirs = before.at[pl.ds(2, 2)]
        remote(theirs, theirs, thr_s, thr_r, sibling).wait_recv()

    def e2():
        beside_landed(1)
        landed(2)
        go(ring(0, (2,), (0, 1)))
        go(ring(2, (3, 1), (0,)))
        go(ring(2, (3, 1), (1,)))
        passed_landed(0)
        pass_copy(1, 1 - core).wait_recv()

    def e3():
        beside_copy(3).start()
        before_copy(1, 1 - core).wait_recv()
        landed(3)
        go(ring(1, (2,), (0, 1)))

    def e5():
        landed(4)
        go(ring(3, (2,), (0, 1)))
        beside_landed(2)

    def e6():
        passed_landed(2)

    def e7():
        landed(5)

    def e8():
        landed(6)
        go(ring(2, (2,), (0, 1)))

    def e9():
        beside_landed(3)

    def e10():
        pass_copy(3, 1 - core).wait_recv()

    def e11():
        before_copy(3, 1 - core).wait_recv()

    def e12():
        landed(7)
        send_gains([(p, 3, dv) for p in (A, B) for dv in (3, 1)] + [(p, 0, 2) for p in (A, B)])

    def e13():
        send_gains([(p, du, 0) for p in (A, B) for du in (0, 1, 3, 2)] + [(p, du, dv) for p in (A, B) for du in (0, 1) for dv in (3, 1)])

    events = {0: e0, 1: e1, 2: e2, 3: e3, 5: e5, 6: e6, 7: e7, 8: e8, 9: e9, 10: e10, 11: e11, 12: e12, 13: e13}

    def prepare(i, low, high):
        if high - low == 1:
            if low in events:
                events[low]()
            return
        middle = (low + high) // 2
        pl.when(i < middle)(functools.partial(prepare, i, low, middle))
        pl.when(i >= middle)(functools.partial(prepare, i, middle, high))

    def product(t, sim):
        group, unit = tile_of(t)
        sim[...] = lax.dot_general(
            pts[pl.ds(pl.multiple_of(unit * UNIT, UNIT), UNIT), :], held[pl.ds(pl.multiple_of(group * GROUP, GROUP), GROUP), :],
            NT, preferred_element_type=jnp.float32)

    def hinge(t, sim):
        group, unit = tile_of(t)
        unit = jnp.where(t < 0, 0, unit)
        slot = jnp.where(t < 0, 4, group)
        for q in range(4):
            sums = [[None] * 6 for _ in range(STEPS)]
            for r in range(16):
                rows = slice(q * BLK + r * 8, q * BLK + r * 8 + 8)
                floors = [before[unit, s, q // 2, q % 2 * BLK + r * 8 : q % 2 * BLK + r * 8 + 8, :] for s in range(3)]
                for c in range(6):
                    value = sim[rows, c * BLK : (c + 1) * BLK]
                    tops = [jnp.maximum(value, 0.0)] + [jnp.maximum(value, floor) for floor in floors]
                    for s in range(STEPS):
                        sums[s][c] = tops[s] if r == 0 else sums[s][c] + tops[s]
            for c in range(6):
                cols = slice(c * BLK, (c + 1) * BLK)
                listed = mask[unit, group, q : q + 1, cols]
                for s in range(STEPS):
                    part = sums[s][c] if s == 0 else sums[s][c] - before[unit, s - 1, q // 2, CHUNK + q % 2 * 8 : CHUNK + q % 2 * 8 + 8, :]
                    acc[slot, s, :, cols] += part * listed

    def pair(i, _):
        t = i * 2
        prepare(i, 0, BLOCKS)
        product(t, sim0)
        hinge(t - 1, sim1)
        product(t + 1, sim1)
        hinge(t, sim0)
        return 0

    lax.fori_loop(0, BLOCKS, pair, 0)
    hinge(jnp.int32(2 * BLOCKS - 1), sim1)
    send_gains([(p, 2, dv) for p in (A, B) for dv in (3, 1)] + [(p, du, 2) for p in (A, B) for du in (1, 3, 2)])

    arrived = got.at[pl.ds(0, 30)]
    remote(arrived, arrived, red_s, red_r, sibling).wait_recv()
    for part in (A, B):
        total = got[part * 16]
        for k in range(1, 16):
            total = total + got[part * 16 + k]
        both[me, part] = total
    for k in range(1, 8):
        last_copy(k, me).start()
    seven = both.at[pl.ds(0, 7)]
    remote(seven, seven, last_s, last_r, sibling).wait_recv()
    for q in range(4):
        for part in (A, B):
            gains[q, part] = (both[q, part] + both[q + 4, part]) / (BLK * PROBES)

    for ref, send, recv in (
        (held.at[pl.ds(0, 60 * HALF)], cand_s, cand_r),
        (pts.at[pl.ds(0, 3 * OWN)], pt_s, pt_r),
        (slots, fac_s, fac_r),
        (columns.at[0], col_s, col_r),
        (lists.at[pl.ds(0, 3)], aux_s, aux_r),
        (before.at[pl.ds(0, 4)], thr_s, thr_r),
        (arrived, red_s, red_r),
        (seven, last_s, last_r),
    ):
        remote(ref, ref, send, recv, sibling).wait_send()


def local(points, candidates, probes, chosen):
    hbm, vmem = pl.BlockSpec(memory_space=pltpu.HBM), pl.BlockSpec(memory_space=pltpu.VMEM)
    f32, bf16, i32 = jnp.float32, jnp.bfloat16, jnp.int32
    dma = pltpu.SemaphoreType.DMA
    listed = jnp.pad(probes, ((0, 0), (0, BLK - PROBES))) + jnp.pad(chosen, (PROBES, BLK - PROBES - STEPS))[None, :]
    gains, cover = pl.pallas_call(
        kernel,
        out_shape=(jax.ShapeDtypeStruct((4, 2, 8, BLK), f32), jax.ShapeDtypeStruct((1, OWN), f32)),
        in_specs=[hbm, hbm, vmem],
        out_specs=(vmem, vmem),
        scratch_shapes=[
            pltpu.VMEM((4 * GROUP, FEATURE), bf16),
            pltpu.VMEM((8 * UNIT, FEATURE), bf16),
            pltpu.VMEM((ROWS, FEATURE // 2), bf16),
            pltpu.VMEM((5, STEPS, 8, GROUP), f32),
            pltpu.VMEM((8, 4, 8, GROUP), f32),
            pltpu.VMEM((8, 3, 2, CHUNK + 16, BLK), f32),
            pltpu.VMEM((UNIT, 3 * BLK), f32),
            pltpu.VMEM((UNIT, GROUP), f32),
            pltpu.VMEM((UNIT, GROUP), f32),
            pltpu.VMEM((4, 8, BLK), i32),
            pltpu.VMEM((4, 8, GROUP), i32),
            pltpu.VMEM((16, 16, BLK), bf16),
            pltpu.VMEM((2, 16, BLK), bf16),
            pltpu.VMEM((3 * BLK, FEATURE), bf16),
            pltpu.VMEM((32, 8, BLK), f32),
            pltpu.VMEM((32, 8, BLK), f32),
            pltpu.VMEM((8, 2, 8, BLK), f32),
            dma((3,)),
            dma((1,)), dma((8,)),
            dma((1,)), dma((1,)),
            dma((1,)), dma((1,)),
            dma((1,)), dma((9,)),
            dma((1,)), dma((3,)),
            dma((1,)), dma((5,)),
            dma((1,)), dma((1,)),
            dma((1,)), dma((1,)),
        ],
        compiler_params=pltpu.CompilerParams(collective_id=0, has_side_effects=True, vmem_limit_bytes=53 << 20),
        name="gather_gain",
    )(points, candidates, listed)
    gains = gains[:, :, :STEPS, :PART].transpose(2, 0, 1, 3).reshape(STEPS, ROWS)
    return (gains, cover.reshape(OWN))


def solution(mesh):
    return jax.shard_map(
        local,
        mesh=mesh,
        in_specs=(P(("pts", "ca", "cb"), None), P(("ca", "cb"), None), P(("pts", "ca", "cb"), None), P()),
        out_specs=(P(None, ("ca", "cb")), P(("pts", "ca", "cb"))),
        check_vma=False,
    )
```
